256 devices in a mesh: tp: 8 (over y_hi, x), cp: 32 (over y_lo, z, core).
Axes of the slice: x: 4, y: 4 (y_hi: 2, y_lo: 2; y = y_hi * 2 + y_lo), z: 8, core: 2. Of those that a mesh axis runs over, the one named last changes fastest.
Arguments:
- inputs: bfloat16 [4096, 4096], P(None, 'cp'), may hold values from -6 to 6
- projected: bfloat16 [3, 4096, 4096], P(None, 'tp', 'cp'), may hold values from -6 to 6
- filters: float32 [4096, 4096], P(('tp', 'cp')), may hold values from -4.5 to 4.5
- grad_out: bfloat16 [4096, 4096], P('tp', 'cp'), may hold values from -6 to 6
Outputs:
- proj_grad: bfloat16 [3, 4096, 4096], P(None, 'tp', 'cp')
- weight_grad: float32 [4096, 3, 4096], P('cp', None, 'tp')
- filter_grad: float32 [4096, 4096], P(('tp', 'cp'))
The draws below stay inside these ranges and needn't reach their ends.
All inputs are finite; a program needn't handle non-finite values.
Results may differ from the reference program's by a relative error of at most 0.013.
Values may be sent and summed in bfloat16 or wider, within the bound.
No kernel may reach another device: no remote copies, remote signals or barrier semaphores. Data moves between devices by JAX's collectives and lax.ppermute only.
A program may use at most 128 MiB of HBM per device.

```python
import jax
import jax.numpy as jnp
from jax import lax

D = 4096
TOKENS = 4096


def draw_filters(key, part):
    key = jax.random.fold_in(key, 11)
    rate_key = jax.random.fold_in(key, 1)
    noise_key = jax.random.fold_in(key, 2)
    length = TOKENS
    log_rate = jax.random.uniform(rate_key, (D, 1), jnp.float32, jnp.log(0.3 / length), jnp.log(1.0 / 30.0))
    noise = jax.random.truncated_normal(noise_key, -4.0, 4.0, (D, length), jnp.float32)
    rate = jnp.exp(log_rate)
    amplitude = jnp.sqrt(2.0 * rate / (1.0 - jnp.exp(-2.0 * rate * length)))
    steps = jnp.arange(length, dtype=jnp.float32)[None, :]
    return (amplitude * jnp.exp(-rate * steps) * noise).astype(jnp.float32)


def spiked(drawn, rng, source, target, blocks, factor):
    def block_of(position):
        return (jnp.arange(drawn.shape[position]) // (drawn.shape[position] // blocks)).reshape((-1,) + (1,) * (drawn.ndim - 1 - position))

    first = jax.random.permutation(rng, blocks)[block_of(target)]
    far = (block_of(target) + blocks // 2) % blocks
    return jnp.where((block_of(source) == first) | (block_of(source) == far), factor * drawn, drawn)


def shard_levels(stream_key, dims, cuts, smallest, largest):
    def one(axis_at, shards_of):
        steps = jax.random.uniform(jax.random.fold_in(jax.random.fold_in(stream_key, 6), axis_at), (shards_of,), jnp.float32, smallest / len(cuts), largest / len(cuts))
        return jnp.repeat(jnp.exp(steps), dims[axis_at] // shards_of).reshape((-1,) + (1,) * (len(dims) - axis_at - 1))

    factor_of = one(*cuts[0])
    for cut in cuts[1:]:
        factor_of = factor_of * one(*cut)
    return factor_of


def gaussian(key, extent, scale, limit, split=(), held_as=jnp.bfloat16):
    values = jax.random.normal(key, extent, jnp.float32) * scale
    if len(split) > 0:
        values = shard_levels(key, extent, split, -0.22, 0.18) * values
    return jnp.clip(values, min=-limit, max=limit).astype(held_as)


def bell_draw_with(own_key, shape, scale, limit, split, heavy, held_as=jnp.bfloat16):
    drawn = scale * jax.random.normal(own_key, shape, jnp.float32)
    if split:
        drawn = drawn * shard_levels(own_key, shape, split, -0.22, 0.18)
    return jnp.clip(spiked(drawn, jax.random.fold_in(own_key, 3), *heavy), -limit, limit).astype(held_as)


def setup_inputs(seed: int = 0) -> dict:
    key_list = jax.random.split(jax.random.key(seed), 5)
    return {
        "inputs": bell_draw_with(key_list[0], (D, TOKENS), 1.0, 6.0, ((1, 32),), (1, 0, 32, 2.75)),
        "projected": gaussian(key_list[1], (3, D, TOKENS), 1.0, 6.0, ((1, 8), (2, 32))),
        "filters": draw_filters(jax.random.fold_in(key_list[4], 71), 0),
        "grad_out": gaussian(key_list[3], (D, TOKENS), 1.0, 6.0, ((0, 8), (1, 32))),
    }


def spectral(block):
    gated_block, carried_block, filter_block = block
    length = filter_block.shape[-1]
    padded = 2 * length
    gated_spec = jnp.fft.rfft(gated_block.astype(jnp.float32), n=padded, axis=-1)
    carried_spec = jnp.fft.rfft(carried_block.astype(jnp.float32), n=padded, axis=-1)
    filter_spec = jnp.fft.rfft(filter_block, n=padded, axis=-1)
    conv = jnp.fft.irfft(filter_spec * gated_spec, n=padded, axis=-1)[:, :length]
    back = jnp.fft.irfft(jnp.conj(filter_spec) * carried_spec, n=padded, axis=-1)[:, :length]
    taps = jnp.fft.irfft(carried_spec * jnp.conj(gated_spec), n=padded, axis=-1)[:, :length]
    return conv, back, taps


def reference(inputs, projected, filters, grad_out):
    query_rows = projected[0].astype(jnp.float32)
    key_rows = projected[1].astype(jnp.float32)
    value_rows = projected[2].astype(jnp.float32)
    gated = (key_rows * value_rows).astype(jnp.bfloat16)
    carried = (grad_out.astype(jnp.float32) * query_rows).astype(jnp.bfloat16)
    length = TOKENS
    count_blocks = 32
    conv, back, taps = lax.map(spectral, (gated.reshape(count_blocks, -1, length), carried.reshape(count_blocks, -1, length), filters.reshape(count_blocks, -1, length)))
    conv = conv.reshape(D, length).astype(jnp.bfloat16).astype(jnp.float32)
    back = back.reshape(D, length).astype(jnp.bfloat16).astype(jnp.float32)
    filter_grad = taps.reshape(D, length)
    proj_grad = jnp.stack([grad_out.astype(jnp.float32) * conv, back * value_rows, back * key_rows]).astype(jnp.bfloat16)
    weight_grad = lax.dot_general(inputs, proj_grad.reshape(3 * D, length), (((1,), (1,)), ((), ())), preferred_element_type=jnp.float32).reshape(D, 3, D)
    return proj_grad, weight_grad, filter_grad
```

```python
import functools
import math

import jax
import jax.numpy as jnp
import ml_dtypes
import numpy as np
from jax import lax
from jax.experimental import pallas as pl
from jax.experimental.pallas import tpu as pltpu
from jax.sharding import Mesh
from jax.sharding import PartitionSpec as P

SEQ = ("ylo", "z", "core")

def halves(table):
    high = table.astype(np.float32).astype(ml_dtypes.bfloat16)
    low = (table - high.astype(np.float64)).astype(np.float32).astype(ml_dtypes.bfloat16)
    return high, low


def tables(blocks, width):
    lead = 2 * blocks
    size = lead * width
    rows = -(-(blocks + 1) // 8) * 8
    k = np.arange(rows, dtype=np.float64)
    live = (k <= blocks).astype(np.float64)
    i = np.arange(blocks, dtype=np.float64)
    j = np.arange(width, dtype=np.float64)
    turn = 2.0 * math.pi * np.outer(k, i) / lead
    lead_fwd = np.concatenate([np.cos(turn) * live[:, None], -np.sin(turn) * live[:, None]], 0)
    weight = np.where((k == 0) | (k == blocks), 1.0, 2.0) * live / size
    lead_inv = np.concatenate([np.cos(turn).T * weight, -np.sin(turn).T * weight], 1)
    twist = 2.0 * math.pi * np.outer(k, j) / size
    tail = 2.0 * math.pi * np.outer(j, j) / width
    cos, sin = np.cos(tail), np.sin(tail)
    tail_fwd = np.block([[cos, -sin], [sin, cos]])
    fh, fl = halves(lead_fwd)
    ih, il = halves(lead_inv)
    th, tl = halves(tail_fwd)
    uh, ul = halves(tail_fwd.T.copy())
    return (
        np.concatenate([fh, fl, fh], 1),
        np.concatenate([ih, il, ih], 1),
        np.cos(twist).astype(np.float32),
        np.sin(twist).astype(np.float32),
        th,
        tl,
        uh,
        ul,
    )


def dot(a, b):
    return jnp.dot(a, b, preferred_element_type=jnp.float32)


def split(x):
    high = x.astype(jnp.bfloat16)
    return high, (x - high.astype(jnp.float32)).astype(jnp.bfloat16)


def kernel(
    chans, width, blocks, pair_ref, filt_ref, lf_ref, li_ref, tc_ref, ts_ref, th_ref, tl_ref, uh_ref, ul_ref, out_ref, grad_ref
):
    rows = tc_ref.shape[0]
    tc, ts = tc_ref[...], ts_ref[...]
    th, tl, uh, ul = th_ref[...], tl_ref[...], uh_ref[...], ul_ref[...]
    lf, li = lf_ref[...], li_ref[...]
    def flat(x):
        return pltpu.einshape("icj->i(cj)", x)
    def forward(high, low):
        if low is None:
            a = dot(lf[:, : 2 * blocks], jnp.concatenate([high, high], 0))
        else:
            a = dot(lf, jnp.concatenate([high, high, low], 0))
        parts = []
        for c in range(chans):
            ar = a[:rows, c * width : (c + 1) * width]
            ai = a[rows:, c * width : (c + 1) * width]
            parts.append(jnp.concatenate([ar * tc + ai * ts, ai * tc - ar * ts], 1))
        high, low = split(jnp.concatenate(parts, 0))
        x = dot(high, th) + dot(low, th) + dot(high, tl)
        return x[:, :width], x[:, width:]
    def inverse(re, im):
        high, low = split(jnp.concatenate([re, im], 1))
        b = dot(high, uh) + dot(low, uh) + dot(high, ul)
        parts = []
        for c in range(chans):
            br = b[c * rows : (c + 1) * rows, :width]
            bi = b[c * rows : (c + 1) * rows, width:]
            parts.append(jnp.concatenate([br * tc - bi * ts, br * ts + bi * tc], 0))
        high, low = split(jnp.concatenate(parts, 1))
        y = dot(li, jnp.concatenate([high, high, low], 0))
        return pltpu.einshape("i(cj)->icj", y, c=chans)
    pair = pair_ref[...]
    gate = flat(pair[:, :chans].astype(jnp.float32)).astype(jnp.bfloat16)
    carr = flat(pair[:, chans:].astype(jnp.float32)).astype(jnp.bfloat16)
    filt = jnp.stack([filt_ref[:, i * width : (i + 1) * width] for i in range(blocks)], 0)
    fr, fi = forward(*split(flat(filt)))
    gr, gi = forward(gate, None)
    cr, ci = forward(carr, None)
    out_ref[:, :chans] = inverse(fr * gr - fi * gi, fr * gi + fi * gr).astype(jnp.bfloat16)
    out_ref[:, chans:] = inverse(fr * cr + fi * ci, fr * ci - fi * cr).astype(jnp.bfloat16)
    taps = inverse(cr * gr + ci * gi, ci * gr - cr * gi)
    for i in range(blocks):
        grad_ref[:, i * width : (i + 1) * width] = taps[i]


def spectral(pair, filters):
    blocks, twice, width = pair.shape
    chans = twice // 2
    return pl.pallas_call(
        functools.partial(kernel, chans, width, blocks),
        out_shape=(jax.ShapeDtypeStruct(pair.shape, jnp.bfloat16), jax.ShapeDtypeStruct(filters.shape, jnp.float32)),
        in_specs=[pl.BlockSpec(memory_space=pltpu.VMEM)] * 10,
        out_specs=[pl.BlockSpec(memory_space=pltpu.VMEM)] * 2,
        compiler_params=pltpu.CompilerParams(vmem_limit_bytes=48 * 1024 * 1024),
    )(pair, filters, *tables(blocks, width))


def swap(x, axis):
    return lax.ppermute(x, axis, [(0, 1), (1, 0)])


def pick(x, index, axis):
    return lax.dynamic_index_in_dim(x, index, axis, keepdims=False)


def exchange_rows(inputs, count_z):
    width = inputs.shape[1]
    y, c = lax.axis_index("ylo"), lax.axis_index("core")
    rows = inputs.shape[0] // (4 * count_z)
    grid = inputs.reshape(2, count_z, 2, rows, width)
    got = swap(pick(grid, 1 - c, 2), "core")
    grid = jnp.concatenate([pick(grid, c, 2), got], -1)
    got = swap(pick(grid, 1 - y, 0), "ylo")
    return jnp.concatenate([pick(grid, y, 0), got], -1)


def gather_near(x):
    x = jnp.concatenate([x, swap(x, "core")], -1)
    return jnp.concatenate([x, swap(x, "ylo")], -1)


def ring_sum(rows, cols, ahead, behind):
    n = rows.shape[0]
    z = lax.axis_index("z")

    def part(k):
        return lax.dot_general(
            pick(rows, lax.rem(k + n, n), 0), cols, (((1,), (1,)), ((), ())), preferred_element_type=jnp.float32
        )

    def arm(hops, way):
        perm = [(i, (i + way) % n) for i in range(n)]
        got = None
        for hop in range(hops, 0, -1):
            total = part(z + way * hop)
            if got is not None:
                total = total + got.astype(jnp.float32)
            got = lax.ppermute(total.astype(jnp.bfloat16), "z", perm)
        return got.astype(jnp.float32)

    up = arm(ahead, 1)
    down = arm(behind, -1)
    return part(z) + up + down


def local(inputs, projected, filters, grad_out):
    chan_width, tok_width = grad_out.shape
    chans = filters.shape[0]
    owners = chan_width // chans
    count_z = lax.axis_size("z")
    query = projected[0].astype(jnp.float32)
    key = projected[1].astype(jnp.float32)
    value = projected[2].astype(jnp.float32)
    out_grad = grad_out.astype(jnp.float32)
    gated = (key * value).astype(jnp.bfloat16).reshape(owners, chans, tok_width)
    carried = (out_grad * query).astype(jnp.bfloat16).reshape(owners, chans, tok_width)
    pair = jnp.concatenate([gated, carried], 1)
    pair = lax.all_to_all(pair, SEQ, split_axis=0, concat_axis=0, tiled=True)
    rows = exchange_rows(inputs, count_z)
    pair, filter_grad = spectral(pair, filters)
    pair = lax.all_to_all(pair, SEQ, split_axis=0, concat_axis=0, tiled=True)
    conv = pair[:, :chans].reshape(chan_width, tok_width).astype(jnp.float32)
    back = pair[:, chans:].reshape(chan_width, tok_width).astype(jnp.float32)
    proj_grad = jnp.stack([out_grad * conv, back * value, back * key]).astype(jnp.bfloat16)
    half = chan_width // 2
    sums = []
    for part in range(2):
        cols = proj_grad[:, part * half : (part + 1) * half].reshape(3 * half, tok_width)
        total = ring_sum(rows, gather_near(cols), count_z // 2 - part, count_z // 2 - 1 + part)
        sums.append(total.reshape(-1, 3, half))
    return proj_grad, jnp.concatenate(sums, 2), filter_grad


def solution(mesh):
    fine = Mesh(mesh.devices.reshape(2, 4, 2, 8, 2), ("yhi", "x", "ylo", "z", "core"))
    tp = ("yhi", "x")
    in_specs = (P(None, SEQ), P(None, tp, SEQ), P(tp + SEQ, None), P(tp, SEQ))
    out_specs = (P(None, tp, SEQ), P(SEQ, None, tp), P(tp + SEQ, None))
    return jax.shard_map(local, mesh=fine, in_specs=in_specs, out_specs=out_specs, check_vma=False)
```

```python
import functools
import math

import jax
import jax.numpy as jnp
import ml_dtypes
import numpy as np
from jax import lax
from jax.experimental import pallas as pl
from jax.experimental.pallas import tpu as pltpu
from jax.sharding import Mesh
from jax.sharding import PartitionSpec as P

SEQ = ("ylo", "z", "core")

def halves(table):
    high = table.astype(np.float32).astype(ml_dtypes.bfloat16)
    low = (table - high.astype(np.float64)).astype(np.float32).astype(ml_dtypes.bfloat16)
    return high, low


def tables(blocks, width):
    lead = 2 * blocks
    size = lead * width
    rows = -(-(blocks + 1) // 8) * 8
    k = np.arange(rows, dtype=np.float64)
    live = (k <= blocks).astype(np.float64)
    i = np.arange(blocks, dtype=np.float64)
    j = np.arange(width, dtype=np.float64)
    turn = 2.0 * math.pi * np.outer(k, i) / lead
    lead_fwd = np.concatenate([np.cos(turn) * live[:, None], -np.sin(turn) * live[:, None]], 0)
    weight = np.where((k == 0) | (k == blocks), 1.0, 2.0) * live / size
    lead_inv = np.concatenate([np.cos(turn).T * weight, -np.sin(turn).T * weight], 1)
    twist = 2.0 * math.pi * np.outer(k, j) / size
    tail = 2.0 * math.pi * np.outer(j, j) / width
    cos, sin = np.cos(tail), np.sin(tail)
    tail_fwd = np.block([[cos, -sin], [sin, cos]])
    fh, fl = halves(lead_fwd)
    ih, il = halves(lead_inv)
    th, tl = halves(tail_fwd)
    uh, ul = halves(tail_fwd.T.copy())
    return (
        np.concatenate([fh, fl, fh], 1),
        np.concatenate([ih, il, ih], 1),
        np.cos(twist).astype(np.float32),
        np.sin(twist).astype(np.float32),
        th,
        tl,
        uh,
        ul,
    )


def dot(a, b):
    return jnp.dot(a, b, preferred_element_type=jnp.float32)


def split(x):
    high = x.astype(jnp.bfloat16)
    return high, (x - high.astype(jnp.float32)).astype(jnp.bfloat16)


def kernel(
    chans, width, blocks, pair_ref, filt_ref, lf_ref, li_ref, tc_ref, ts_ref, th_ref, tl_ref, uh_ref, ul_ref, out_ref, grad_ref
):
    rows = tc_ref.shape[0]
    tc, ts = tc_ref[...], ts_ref[...]
    th, tl, uh, ul = th_ref[...], tl_ref[...], uh_ref[...], ul_ref[...]
    lf, li = lf_ref[...], li_ref[...]
    def flat(x):
        return pltpu.einshape("icj->i(cj)", x)
    def forward(high, low):
        if low is None:
            a = dot(lf[:, : 2 * blocks], jnp.concatenate([high, high], 0))
        else:
            a = dot(lf, jnp.concatenate([high, high, low], 0))
        parts = []
        for c in range(chans):
            ar = a[:rows, c * width : (c + 1) * width]
            ai = a[rows:, c * width : (c + 1) * width]
            parts.append(jnp.concatenate([ar * tc + ai * ts, ai * tc - ar * ts], 1))
        high, low = split(jnp.concatenate(parts, 0))
        x = dot(high, th) + dot(low, th) + dot(high, tl)
        return x[:, :width], x[:, width:]
    def inverse(re, im):
        high, low = split(jnp.concatenate([re, im], 1))
        b = dot(high, uh) + dot(low, uh) + dot(high, ul)
        parts = []
        for c in range(chans):
            br = b[c * rows : (c + 1) * rows, :width]
            bi = b[c * rows : (c + 1) * rows, width:]
            parts.append(jnp.concatenate([br * tc - bi * ts, br * ts + bi * tc], 0))
        high, low = split(jnp.concatenate(parts, 1))
        y = dot(li, jnp.concatenate([high, high, low], 0))
        return pltpu.einshape("i(cj)->icj", y, c=chans)
    pair = pair_ref[...]
    gate = flat(pair[:, :chans].astype(jnp.float32)).astype(jnp.bfloat16)
    carr = flat(pair[:, chans:].astype(jnp.float32)).astype(jnp.bfloat16)
    filt = jnp.stack([filt_ref[:, i * width : (i + 1) * width] for i in range(blocks)], 0)
    fr, fi = forward(*split(flat(filt)))
    gr, gi = forward(gate, None)
    cr, ci = forward(carr, None)
    out_ref[:, :chans] = inverse(fr * gr - fi * gi, fr * gi + fi * gr).astype(jnp.bfloat16)
    out_ref[:, chans:] = inverse(fr * cr + fi * ci, fr * ci - fi * cr).astype(jnp.bfloat16)
    taps = inverse(cr * gr + ci * gi, ci * gr - cr * gi)
    for i in range(blocks):
        grad_ref[:, i * width : (i + 1) * width] = taps[i]


def spectral(pair, filters):
    blocks, twice, width = pair.shape
    chans = twice // 2
    return pl.pallas_call(
        functools.partial(kernel, chans, width, blocks),
        out_shape=(jax.ShapeDtypeStruct(pair.shape, jnp.bfloat16), jax.ShapeDtypeStruct(filters.shape, jnp.float32)),
        in_specs=[pl.BlockSpec(memory_space=pltpu.VMEM)] * 10,
        out_specs=[pl.BlockSpec(memory_space=pltpu.VMEM)] * 2,
        compiler_params=pltpu.CompilerParams(vmem_limit_bytes=48 * 1024 * 1024),
    )(pair, filters, *tables(blocks, width))


def vmem_call(body, outs, *args):
    return pl.pallas_call(
        body,
        out_shape=tuple(jax.ShapeDtypeStruct(shape, dtype) for shape, dtype in outs),
        in_specs=[pl.BlockSpec(memory_space=pltpu.VMEM)] * len(args),
        out_specs=tuple(pl.BlockSpec(memory_space=pltpu.VMEM) for _ in outs),
        compiler_params=pltpu.CompilerParams(vmem_limit_bytes=48 * 1024 * 1024),
    )(*args)


def gate_kernel(owners, chans, projected_ref, grad_ref, pair_ref):
    width = grad_ref.shape[1]
    query, key, value = (projected_ref[s].astype(jnp.float32) for s in range(3))
    gated = (key * value).astype(jnp.bfloat16)
    carried = (grad_ref[...].astype(jnp.float32) * query).astype(jnp.bfloat16)
    pair_ref[:, :chans] = gated.reshape(owners, chans, width)
    pair_ref[:, chans:] = carried.reshape(owners, chans, width)


def grad_kernel(chans, pair_ref, projected_ref, grad_ref, out_ref, low_ref, high_ref):
    count, width = grad_ref.shape
    conv = pair_ref[:, :chans].reshape(count, width).astype(jnp.float32)
    back = pair_ref[:, chans:].reshape(count, width).astype(jnp.float32)
    first = (grad_ref[...].astype(jnp.float32) * conv).astype(jnp.bfloat16)
    second = (back * projected_ref[2].astype(jnp.float32)).astype(jnp.bfloat16)
    third = (back * projected_ref[1].astype(jnp.float32)).astype(jnp.bfloat16)
    out_ref[0] = first
    out_ref[1] = second
    out_ref[2] = third
    low_ref[:count] = first
    low_ref[count:] = second[: count // 2]
    high_ref[: count // 2] = second[count // 2 :]
    high_ref[count // 2 :] = third


def product_kernel(rows_ref, a_ref, b_ref, c_ref, d_ref, out_ref):
    cols = jnp.concatenate([a_ref[...], b_ref[...], c_ref[...], d_ref[...]], 1)
    out_ref[...] = lax.dot_general(
        rows_ref[...], cols, (((1,), (1,)), ((), ())), preferred_element_type=jnp.float32
    ).astype(jnp.bfloat16)


def finish_kernel(count, *refs):
    sums = [sum(ref[...].astype(jnp.float32) for ref in refs[3 * k : 3 * k + 3]) for k in range(2)]
    out_ref = refs[6]
    half = count // 2
    out_ref[0] = sums[0][:, :count]
    out_ref[1, :, :half] = sums[0][:, count:]
    out_ref[1, :, half:] = sums[1][:, :half]
    out_ref[2] = sums[1][:, half:]


def swap(x, axis):
    return lax.ppermute(x, axis, [(0, 1), (1, 0)])


def pick(x, index, axis):
    return lax.dynamic_index_in_dim(x, index, axis, keepdims=False)


def after(x, *others):
    return lax.optimization_barrier((x, *others))[0]


def near_blocks(x):
    beside = swap(x, "ylo")
    return x, beside, swap(x, "core"), swap(beside, "core")


def add(x, y):
    return (x.astype(jnp.float32) + y.astype(jnp.float32)).astype(jnp.bfloat16)


def ring_sums(owns, n):
    z = lax.axis_index("z")
    ways = (1, -1)
    hops = [[n // 2 - (k % 2), n // 2 - 1 + (k % 2)] for k in range(len(owns))]
    got = [[None, None] for _ in owns]
    last = None
    for turn in range(n // 2):
        for k, own in enumerate(owns):
            totals = []
            for w, way in enumerate(ways):
                hop = hops[k][w] - turn
                if hop < 1:
                    continue
                total = pick(own, lax.rem(z + way * hop + n, n), 0)
                if got[k][w] is not None:
                    total = add(total, got[k][w])
                totals.append((w, total))
            if last is not None:
                fixed = lax.optimization_barrier((*[t for _, t in totals], last))
                totals = [(w, fixed[m]) for m, (w, _) in enumerate(totals)]
            last = totals[0][1]
            for w, total in totals:
                perm = [(i, (i + ways[w]) % n) for i in range(n)]
                got[k][w] = lax.ppermute(total, "z", perm)
    return [x for k, own in enumerate(owns) for x in (pick(own, z, 0), *got[k])]


def local(inputs, projected, filters, grad_out):
    count, width = grad_out.shape
    chans = filters.shape[0]
    owners = count // chans
    n = lax.axis_size("z")
    y, c = lax.axis_index("ylo"), lax.axis_index("core")
    bf16 = jnp.bfloat16

    rows = inputs.shape[0] // (4 * n)
    grid = inputs.reshape(2, n, 2, rows, width)
    beside = swap(pick(grid, 1 - y, 0), "ylo")
    (pair,) = vmem_call(
        functools.partial(gate_kernel, owners, chans), [((owners, 2 * chans, width), bf16)], projected, grad_out
    )
    pair = lax.all_to_all(pair, SEQ, split_axis=0, concat_axis=0, tiled=True)
    pair, beside = lax.optimization_barrier((pair, beside))
    grid = jnp.concatenate([pick(grid, y, 0), beside], -1)
    far = swap(pick(grid, 1 - c, 1), "core")
    pair, filter_grad = spectral(pair, filters)
    rows_near = jnp.concatenate([pick(grid, c, 1), far], -1).reshape(n * rows, 4 * width)

    pair = lax.all_to_all(pair, SEQ, split_axis=0, concat_axis=0, tiled=True)
    half = 3 * count // 2
    proj_grad, low, high = vmem_call(
        functools.partial(grad_kernel, chans),
        [((3, count, width), bf16), ((half, width), bf16), ((half, width), bf16)],
        pair,
        projected,
        grad_out,
    )
    owns = []
    for cols in (low, high):
        (own,) = vmem_call(product_kernel, [((n * rows, half), bf16)], rows_near, *near_blocks(cols))
        owns.append(own.reshape(n, rows, half))
    (weight_grad,) = vmem_call(
        functools.partial(finish_kernel, count), [((3, rows, count), jnp.float32)], *ring_sums(owns, n)
    )
    return proj_grad, weight_grad.transpose(1, 0, 2), filter_grad


def solution(mesh):
    fine = Mesh(mesh.devices.reshape(2, 4, 2, 8, 2), ("yhi", "x", "ylo", "z", "core"))
    tp = ("yhi", "x")
    in_specs = (P(None, SEQ), P(None, tp, SEQ), P(tp + SEQ, None), P(tp, SEQ))
    out_specs = (P(None, tp, SEQ), P(SEQ, None, tp), P(tp + SEQ, None))
    return jax.shard_map(local, mesh=fine, in_specs=in_specs, out_specs=out_specs, check_vma=False)
```

```python
import functools
import math

import jax
import jax.numpy as jnp
import ml_dtypes
import numpy as np
from jax import lax
from jax.experimental import pallas as pl
from jax.experimental.pallas import tpu as pltpu
from jax.sharding import Mesh
from jax.sharding import PartitionSpec as P

SEQ = ("ylo", "z", "core")

def halves(table):
    high = table.astype(np.float32).astype(ml_dtypes.bfloat16)
    low = (table - high.astype(np.float64)).astype(np.float32).astype(ml_dtypes.bfloat16)
    return high, low


def tables(blocks, width):
    lead = 2 * blocks
    size = lead * width
    rows = -(-(blocks + 1) // 8) * 8
    k = np.arange(rows, dtype=np.float64)
    live = (k <= blocks).astype(np.float64)
    i = np.arange(blocks, dtype=np.float64)
    j = np.arange(width, dtype=np.float64)
    turn = 2.0 * math.pi * np.outer(k, i) / lead
    lead_fwd = np.concatenate([np.cos(turn) * live[:, None], -np.sin(turn) * live[:, None]], 0)
    weight = np.where((k == 0) | (k == blocks), 1.0, 2.0) * live / size
    lead_inv = np.concatenate([np.cos(turn).T * weight, -np.sin(turn).T * weight], 1)
    twist = 2.0 * math.pi * np.outer(k, j) / size
    tail = 2.0 * math.pi * np.outer(j, j) / width
    cos, sin = np.cos(tail), np.sin(tail)
    tail_fwd = np.block([[cos, -sin], [sin, cos]])
    fh, fl = halves(lead_fwd)
    ih, il = halves(lead_inv)
    th, tl = halves(tail_fwd)
    uh, ul = halves(tail_fwd.T.copy())
    return (
        np.concatenate([fh, fl, fh], 1),
        np.concatenate([ih, il, ih], 1),
        np.cos(twist).astype(np.float32),
        np.sin(twist).astype(np.float32),
        th,
        tl,
        uh,
        ul,
    )


def dot(a, b):
    return jnp.dot(a, b, preferred_element_type=jnp.float32)


def split(x):
    high = x.astype(jnp.bfloat16)
    return high, (x - high.astype(jnp.float32)).astype(jnp.bfloat16)


def kernel(
    chans, width, blocks, sent_ref, filt_ref, lf_ref, li_ref, tc_ref, ts_ref, th_ref, tl_ref, uh_ref, ul_ref, out_ref, taps_ref
):
    rows = tc_ref.shape[0]
    tc, ts = tc_ref[...], ts_ref[...]
    th, tl, uh, ul = th_ref[...], tl_ref[...], uh_ref[...], ul_ref[...]
    lf, li = lf_ref[...], li_ref[...]

    def flat(x):
        return pltpu.einshape("icj->i(cj)", x)

    def forward(high, low):
        if low is None:
            a = dot(lf[:, : 2 * blocks], jnp.concatenate([high, high], 0))
        else:
            a = dot(lf, jnp.concatenate([high, high, low], 0))
        parts = []
        for c in range(chans):
            ar = a[:rows, c * width : (c + 1) * width]
            ai = a[rows:, c * width : (c + 1) * width]
            parts.append(jnp.concatenate([ar * tc + ai * ts, ai * tc - ar * ts], 1))
        high, low = split(jnp.concatenate(parts, 0))
        x = dot(high, th) + dot(low, th) + dot(high, tl)
        return x[:, :width], x[:, width:]

    def inverse(re, im):
        high, low = split(jnp.concatenate([re, im], 1))
        b = dot(high, uh) + dot(low, uh) + dot(high, ul)
        parts = []
        for c in range(chans):
            br = b[c * rows : (c + 1) * rows, :width]
            bi = b[c * rows : (c + 1) * rows, width:]
            parts.append(jnp.concatenate([br * tc - bi * ts, br * ts + bi * tc], 0))
        high, low = split(jnp.concatenate(parts, 1))
        y = dot(li, jnp.concatenate([high, high, low], 0))
        return pltpu.einshape("i(cj)->icj", y, c=chans)

    def stream(s):
        return sent_ref[:, s * chans : (s + 1) * chans].astype(jnp.float32)

    def put(s, x):
        half = blocks // 2
        for i in range(blocks):
            at = i % half
            out_ref[i // half, s * chans : (s + 1) * chans, at * width : (at + 1) * width] = x[i].astype(jnp.bfloat16)

    gate = flat((stream(1) * stream(2)).astype(jnp.bfloat16).astype(jnp.float32)).astype(jnp.bfloat16)
    carr = flat((stream(3) * stream(0)).astype(jnp.bfloat16).astype(jnp.float32)).astype(jnp.bfloat16)
    filt = jnp.stack([filt_ref[:, i * width : (i + 1) * width] for i in range(blocks)], 0)
    fr, fi = forward(*split(flat(filt)))
    gr, gi = forward(gate, None)
    cr, ci = forward(carr, None)
    conv = inverse(fr * gr - fi * gi, fr * gi + fi * gr).astype(jnp.bfloat16).astype(jnp.float32)
    put(0, stream(3) * conv)
    back = inverse(fr * cr + fi * ci, fr * ci - fi * cr).astype(jnp.bfloat16).astype(jnp.float32)
    put(1, back * stream(2))
    put(2, back * stream(1))
    taps = inverse(cr * gr + ci * gi, ci * gr - cr * gi)
    for i in range(blocks):
        taps_ref[:, i * width : (i + 1) * width] = taps[i]


def vmem_call(body, outs, *args, scratch=(), place=None):
    specs = [pl.BlockSpec(memory_space=pltpu.VMEM)] * len(args)
    if place is not None:
        specs = [pl.BlockSpec(memory_space=pltpu.SMEM)] + specs
        args = (place,) + args
    return pl.pallas_call(
        body,
        out_shape=tuple(jax.ShapeDtypeStruct(shape, dtype) for shape, dtype in outs),
        in_specs=specs,
        out_specs=tuple(pl.BlockSpec(memory_space=pltpu.VMEM) for _ in outs),
        scratch_shapes=scratch,
        compiler_params=pltpu.CompilerParams(vmem_limit_bytes=48 * 1024 * 1024),
    )(*args)


def spectral(sent, filters):
    blocks, _, width = sent.shape
    chans = filters.shape[0]
    return vmem_call(
        functools.partial(kernel, chans, width, blocks),
        [((2, 3 * chans, blocks * width // 2), jnp.bfloat16), (filters.shape, jnp.float32)],
        sent,
        filters,
        *tables(blocks, width),
    )


def pack_kernel(chans, place_ref, inputs_ref, projected_ref, grad_ref, out_ref):
    owners, _, rows, width = inputs_ref.shape
    for s in range(3):
        out_ref[:, s * chans : (s + 1) * chans] = projected_ref[s].reshape(owners, chans, width)
    out_ref[:, 3 * chans : 4 * chans] = grad_ref[...].reshape(owners, chans, width)
    out_ref[:, 4 * chans :] = inputs_ref[:, place_ref[3]]


def rows_kernel(place_ref, *refs):
    x = place_ref[3]
    for refs, out_ref in ((refs[:5], refs[10]), (refs[5:10], refs[11])):
        own_ref, up_ref, down_ref, first_ref, second_ref = refs
        _, blocks, rows, width = own_ref.shape
        count = out_ref.shape[1] // rows
        for shift, parts in (
            (0, (own_ref[0], own_ref[1])),
            (count - 1, (up_ref[0], up_ref[1])),
            (1, (down_ref[0], down_ref[1])),
            (2, (first_ref[...], second_ref[...])),
        ):
            at = pl.multiple_of(lax.rem(x + shift, count) * rows, rows)
            for y in range(2):
                for i in range(blocks):
                    out_ref[y, pl.ds(at, rows), i * width : (i + 1) * width] = parts[y][i]


def product_kernel(split_last, place_ref, near_ref, far_ref, *refs):
    blocks, outs = refs[:-4], refs[-4:]
    y, z, c = place_ref[0], place_ref[1], place_ref[2]
    if split_last:
        halves = [[r[h] for r in blocks[:-2]] + [blocks[-2 + h][...]] for h in range(2)]
    else:
        halves = [[r[h] for r in blocks] for h in range(2)]
    halves = [jnp.concatenate(h, 0) for h in halves]
    length = halves[0].shape[1]
    rows = halves[0].shape[0]
    width = near_ref.shape[1]
    whole = blocks[:-2] if split_last else blocks
    count = rows // (len(whole) + (1 if split_last else 0))
    for rc, ref in enumerate((near_ref, far_ref)):
        total = None
        for h in range(2):
            x = jnp.concatenate([ref[0, :, h * length : (h + 1) * length], ref[1, :, h * length : (h + 1) * length]], 0)
            part = lax.dot_general(halves[h], x, (((1,), (1,)), ((), ())), preferred_element_type=jnp.float32)
            total = part if total is None else total + part
        total = total.astype(jnp.bfloat16)
        for ry in range(2):
            out_ref = outs[2 * ry + rc]
            out_ref[:rows] = total[:, ry * width : (ry + 1) * width]
            half = lax.rem(y + ry, 2)
            at = pl.multiple_of((2 * z + lax.rem(c + rc, 2)) * width, width)
            for k, ref_k in enumerate(whole):
                out_ref[rows + k * count : rows + (k + 1) * count] = ref_k[half, :, pl.ds(at, width)]
            if split_last:

                @pl.when(half == 0)
                def _():
                    out_ref[2 * rows - count :] = blocks[-2][:, pl.ds(at, width)]

                @pl.when(half == 1)
                def _():
                    out_ref[2 * rows - count :] = blocks[-1][:, pl.ds(at, width)]


def finish_kernel(chans, n, shifts, place_ref, *refs):
    groups, (proj_ref, weight_ref, turned_ref) = refs[:-3], refs[-3:]
    y, z, c = place_ref[0], place_ref[1], place_ref[2]
    for g, shift_list in enumerate(shifts):
        rows = 3 * chans * len(shift_list)
        for near in range(4):
            ref = groups[4 * g + near]
            there = lax.rem(y + near // 2, 2) * 2 * n + lax.rem(c + near % 2, 2)
            for m, shift in enumerate(shift_list):
                at = pl.multiple_of((there + 2 * lax.rem(z + shift, n)) * chans, chans)
                for s in range(3):
                    row = (3 * m + s) * chans
                    turned_ref[s, pl.ds(at, chans), :] = ref[row : row + chans, :].astype(jnp.float32)
                    proj_ref[s, pl.ds(at, chans), :] = ref[rows + row : rows + row + chans, :]
    for s in range(3):
        weight_ref[s] = turned_ref[s].T


def shift_by(x, axis, way):
    n = lax.axis_size(axis)
    return lax.ppermute(x, axis, [(i, (i + way) % n) for i in range(n)])


def swap(x, axis):
    return lax.ppermute(x, axis, [(0, 1), (1, 0)])


def after(x, *others):
    return lax.optimization_barrier((x, *others))[0]


def trade(parts):
    across = lax.ppermute(parts[3], ("ylo", "core"), [(0, 3), (1, 2), (2, 1), (3, 0)])
    return parts[0], swap(parts[1], "core"), swap(parts[2], "ylo"), across


def local(inputs, projected, filters, grad_out):
    count, width = grad_out.shape
    chans = filters.shape[0]
    owners = count // chans
    n = lax.axis_size("z")
    n_x = lax.axis_size("x")
    bf16 = jnp.bfloat16
    place = jnp.stack([lax.axis_index(a) for a in ("ylo", "z", "core", "x")]).astype(jnp.int32)
    rows = inputs.shape[0] // (owners * n_x)

    (sent,) = vmem_call(
        functools.partial(pack_kernel, chans),
        [((owners, 4 * chans + rows, width), bf16)],
        inputs.reshape(owners, n_x, rows, width),
        projected,
        grad_out,
        place=place,
    )
    sent = lax.all_to_all(sent, SEQ, split_axis=0, concat_axis=0, tiled=True)
    own_rows = sent[:, 4 * chans :]
    both_rows = jnp.stack([own_rows, swap(own_rows, "ylo")])

    block, filter_grad = spectral(sent, filters)
    up1, down1 = shift_by(block, "z", 1), shift_by(block, "z", -1)
    both_rows = after(both_rows, block)
    x_up, x_down = shift_by(both_rows, "x", 1), shift_by(both_rows, "x", -1)
    up1, down1, both_rows = lax.optimization_barrier((up1, down1, both_rows))
    up2, down2 = shift_by(up1, "z", 1), shift_by(down1, "z", -1)
    x_up, x_down, up1, down1 = lax.optimization_barrier((x_up, x_down, up1, down1))
    x_first, x_second = shift_by(x_up[0], "x", 1), shift_by(x_down[1], "x", -1)
    up2, down2, x_up, x_down = lax.optimization_barrier((up2, down2, x_up, x_down))
    up3, down3 = shift_by(up2, "z", 1), shift_by(down2, "z", -1)
    pieces = (both_rows, x_up, x_down, x_first, x_second)
    pieces = (*pieces, *(swap(p, "core") for p in pieces))
    near_rows, far_rows = vmem_call(
        rows_kernel, [((2, n_x * rows, owners * width), bf16)] * 2, *pieces, place=place
    )
    near_rows, far_rows, up3, down3 = lax.optimization_barrier((near_rows, far_rows, up3, down3))
    up4, down4 = shift_by(up3[0], "z", 1), shift_by(down3[1], "z", -1)

    shifts = ((0, n - 1, 1, n - 2, 2), (n - 3, 3, n // 2))
    groups = []
    for k, blocks in enumerate(((block, up1, down1, up2, down2), (up3, down3, up4, down4))):
        if groups:
            blocks = lax.optimization_barrier((*blocks, *groups[:1]))[:-1]
        size = 6 * chans * len(shifts[k])
        parts = vmem_call(
            functools.partial(product_kernel, k == 1),
            [((size, width), bf16)] * 4,
            near_rows,
            far_rows,
            *blocks,
            place=place,
        )
        groups += trade(parts)
    proj_grad, weight_grad = vmem_call(
        functools.partial(finish_kernel, chans, n, shifts),
        [((3, count, width), bf16), ((3, n_x * rows, count), jnp.float32)],
        *groups,
        scratch=[pltpu.VMEM((3, count, width), jnp.float32)],
        place=place,
    )
    return proj_grad, weight_grad.transpose(1, 0, 2), filter_grad


def solution(mesh):
    fine = Mesh(mesh.devices.reshape(2, 4, 2, 8, 2), ("yhi", "x", "ylo", "z", "core"))
    tp = ("yhi", "x")
    in_specs = (P(None, SEQ), P(None, tp, SEQ), P(tp + SEQ, None), P(tp, SEQ))
    out_specs = (P(None, tp, SEQ), P(SEQ, None, tp), P(tp + SEQ, None))
    return jax.shard_map(local, mesh=fine, in_specs=in_specs, out_specs=out_specs, check_vma=False)
```

```python
import functools
import math

import jax
import jax.numpy as jnp
import ml_dtypes
import numpy as np
from jax import lax
from jax.experimental import pallas as pl
from jax.experimental.pallas import tpu as pltpu
from jax.sharding import Mesh
from jax.sharding import PartitionSpec as P

SEQ = ("ylo", "z", "core")

def halves(table):
    high = table.astype(np.float32).astype(ml_dtypes.bfloat16)
    low = (table - high.astype(np.float64)).astype(np.float32).astype(ml_dtypes.bfloat16)
    return high, low


def tables(blocks, width):
    lead = 2 * blocks
    size = lead * width
    rows = -(-(blocks + 1) // 8) * 8
    k = np.arange(rows, dtype=np.float64)
    live = (k <= blocks).astype(np.float64)
    i = np.arange(blocks, dtype=np.float64)
    j = np.arange(width, dtype=np.float64)
    turn = 2.0 * math.pi * np.outer(k, i) / lead
    lead_fwd = np.concatenate([np.cos(turn) * live[:, None], -np.sin(turn) * live[:, None]], 0)
    weight = np.where((k == 0) | (k == blocks), 1.0, 2.0) * live / size
    lead_inv = np.concatenate([np.cos(turn).T * weight, -np.sin(turn).T * weight], 1)
    twist = 2.0 * math.pi * np.outer(k, j) / size
    tail = 2.0 * math.pi * np.outer(j, j) / width
    cos, sin = np.cos(tail), np.sin(tail)
    tail_fwd = np.block([[cos, -sin], [sin, cos]])
    fh, fl = halves(lead_fwd)
    ih, il = halves(lead_inv)
    th, tl = halves(tail_fwd)
    uh, ul = halves(tail_fwd.T.copy())
    return (
        np.concatenate([fh, fl, fh], 1),
        np.concatenate([ih, il, ih], 1),
        np.cos(twist).astype(np.float32),
        np.sin(twist).astype(np.float32),
        th,
        tl,
        uh,
        ul,
    )


def dot(a, b):
    return jnp.dot(a, b, preferred_element_type=jnp.float32)


def split(x):
    high = x.astype(jnp.bfloat16)
    return high, (x - high.astype(jnp.float32)).astype(jnp.bfloat16)


def kernel(
    chans, width, blocks, sent_ref, filt_ref, lf_ref, li_ref, tc_ref, ts_ref, th_ref, tl_ref, uh_ref, ul_ref, out_ref, taps_ref
):
    rows = tc_ref.shape[0]
    tc, ts = tc_ref[...], ts_ref[...]
    th, tl, uh, ul = th_ref[...], tl_ref[...], uh_ref[...], ul_ref[...]
    lf, li = lf_ref[...], li_ref[...]

    def flat(x):
        return pltpu.einshape("icj->i(cj)", x)

    def forward(high, low):
        if low is None:
            a = dot(lf[:, : 2 * blocks], jnp.concatenate([high, high], 0))
        else:
            a = dot(lf, jnp.concatenate([high, high, low], 0))
        parts = []
        for c in range(chans):
            ar = a[:rows, c * width : (c + 1) * width]
            ai = a[rows:, c * width : (c + 1) * width]
            parts.append(jnp.concatenate([ar * tc + ai * ts, ai * tc - ar * ts], 1))
        high, low = split(jnp.concatenate(parts, 0))
        x = dot(high, th) + dot(low, th) + dot(high, tl)
        return x[:, :width], x[:, width:]

    def inverse(re, im):
        high, low = split(jnp.concatenate([re, im], 1))
        b = dot(high, uh) + dot(low, uh) + dot(high, ul)
        parts = []
        for c in range(chans):
            br = b[c * rows : (c + 1) * rows, :width]
            bi = b[c * rows : (c + 1) * rows, width:]
            parts.append(jnp.concatenate([br * tc - bi * ts, br * ts + bi * tc], 0))
        high, low = split(jnp.concatenate(parts, 1))
        y = dot(li, jnp.concatenate([high, high, low], 0))
        return pltpu.einshape("i(cj)->icj", y, c=chans)

    def stream(s):
        return sent_ref[:, s * chans : (s + 1) * chans].astype(jnp.float32)

    def put(s, x):
        half = blocks // 2
        for i in range(blocks):
            at = i % half
            out_ref[i // half, s * chans : (s + 1) * chans, at * width : (at + 1) * width] = x[i].astype(jnp.bfloat16)

    gate = flat((stream(1) * stream(2)).astype(jnp.bfloat16).astype(jnp.float32)).astype(jnp.bfloat16)
    carr = flat((stream(3) * stream(0)).astype(jnp.bfloat16).astype(jnp.float32)).astype(jnp.bfloat16)
    filt = jnp.stack([filt_ref[:, i * width : (i + 1) * width] for i in range(blocks)], 0)
    fr, fi = forward(*split(flat(filt)))
    gr, gi = forward(gate, None)
    cr, ci = forward(carr, None)
    conv = inverse(fr * gr - fi * gi, fr * gi + fi * gr).astype(jnp.bfloat16).astype(jnp.float32)
    put(0, stream(3) * conv)
    back = inverse(fr * cr + fi * ci, fr * ci - fi * cr).astype(jnp.bfloat16).astype(jnp.float32)
    put(1, back * stream(2))
    put(2, back * stream(1))
    taps = inverse(cr * gr + ci * gi, ci * gr - cr * gi)
    for i in range(blocks):
        taps_ref[:, i * width : (i + 1) * width] = taps[i]


def vmem_call(body, outs, *args, scratch=(), place=None):
    specs = [pl.BlockSpec(memory_space=pltpu.VMEM)] * len(args)
    if place is not None:
        specs = [pl.BlockSpec(memory_space=pltpu.SMEM)] + specs
        args = (place,) + args
    return pl.pallas_call(
        body,
        out_shape=tuple(jax.ShapeDtypeStruct(shape, dtype) for shape, dtype in outs),
        in_specs=specs,
        out_specs=tuple(pl.BlockSpec(memory_space=pltpu.VMEM) for _ in outs),
        scratch_shapes=scratch,
        compiler_params=pltpu.CompilerParams(vmem_limit_bytes=24 * 1024 * 1024),
    )(*args)


def spectral(sent, filters):
    blocks, _, width = sent.shape
    chans = filters.shape[0]
    return vmem_call(
        functools.partial(kernel, chans, width, blocks),
        [((2, 3 * chans, blocks * width // 2), jnp.bfloat16), (filters.shape, jnp.float32)],
        sent,
        filters,
        *tables(blocks, width),
    )


def pack_kernel(chans, inputs_ref, projected_ref, grad_ref, out_ref, sems):
    copies = [
        pltpu.make_async_copy(projected_ref.at[s], out_ref.at[:, s * chans : (s + 1) * chans], sems.at[s])
        for s in range(3)
    ]
    copies.append(pltpu.make_async_copy(grad_ref, out_ref.at[:, 3 * chans : 4 * chans], sems.at[3]))
    copies.append(pltpu.make_async_copy(inputs_ref.at[:, lax.axis_index("x")], out_ref.at[:, 4 * chans :], sems.at[4]))
    for copy in copies:
        copy.start()
    for copy in copies:
        copy.wait()


def chunk(place_ref, blocks, ry, rc):
    y, z, c = place_ref[0], place_ref[1], place_ref[2]
    half = lax.rem(y + ry, 2)
    at = pl.multiple_of((2 * z + lax.rem(c + rc, 2)) * 128, 128)
    return jnp.concatenate([block[half, :, pl.ds(at, 128)] for block in blocks], 0)


def chunk_kernel(place_ref, *refs):
    blocks, outs = refs[:-4], refs[-4:]
    for near, out_ref in enumerate(outs):
        out_ref[...] = chunk(place_ref, blocks, near // 2, near % 2)


def product_kernel(with_chunks, place_ref, *refs):
    own, first, second, third, other, other_first, other_second, other_third = refs[:8]
    blocks, outs = refs[8:-4], refs[-4:]
    halves = [jnp.concatenate([block[h] for block in blocks], 0) for h in range(2)]
    rows, length = halves[0].shape
    _, steps, part, width = own.shape
    size = 4 * part
    for rc, pieces in enumerate(((own, first, third, other_second), (other, second, other_third, other_first))):
        total = None
        for h in range(2):
            span = range(h * steps // 2, (h + 1) * steps // 2)
            x = jnp.concatenate(
                [jnp.concatenate([ref[y, i] for i in span], 1) for y in range(2) for ref in pieces], 0
            )
            got = lax.dot_general(halves[h], x, (((1,), (1,)), ((), ())), preferred_element_type=jnp.float32)
            total = got if total is None else total + got
        for ry in range(2):
            t = total[:, ry * size : (ry + 1) * size]
            u = jnp.concatenate([t[:, :part], t[:, 3 * part :], t[:, 2 * part : 3 * part], t[:, part : 2 * part]], 1)
            out_ref = outs[2 * ry + rc]
            out_ref[:rows] = jnp.where(place_ref[2] == 0, u, t).astype(jnp.bfloat16)
            if with_chunks:
                out_ref[rows:] = chunk(place_ref, blocks, ry, rc)


def finish_kernel(chans, n, slots, place_ref, *refs):
    groups, (proj_ref, weight_ref, turned_ref) = refs[:-3], refs[-3:]
    y, z, c, x = (place_ref[k] for k in range(4))
    for g, slot_list in enumerate(slots):
        rows = 3 * chans * len(slot_list)
        for near in range(4):
            weights = groups[8 * g + near]
            chunks, base = (groups[4 + near], 0) if g == 0 else (weights, rows)
            core = lax.rem(c + near % 2, 2)
            row_y = lax.rem(y + near // 2, 2) * 2 * n
            for m, (hops, turned) in enumerate(slot_list):
                owner = row_y + 2 * lax.rem(z + n - hops + 2 * hops * core, n) + (1 - core if turned else core)
                at = pl.multiple_of(owner * chans, chans)
                for s in range(3):
                    row = (3 * m + s) * chans
                    turned_ref[s, pl.ds(at, chans), :] = weights[row : row + chans, :].astype(jnp.float32)
                    proj_ref[s, pl.ds(at, chans), :] = chunks[base + row : base + row + chans, :]
    n_x = 4
    part = weight_ref.shape[1] // n_x
    for s in range(3):
        rows = turned_ref[s].T
        for k in range(n_x):
            at = pl.multiple_of(lax.rem(x + k, n_x) * part, part)
            weight_ref[s, pl.ds(at, part), :] = rows[k * part : (k + 1) * part]


def spread(x, axis):
    n = lax.axis_size(axis)
    perm = [(2 * i, 2 * ((i + 1) % n)) for i in range(n)] + [(2 * i + 1, 2 * ((i + n - 1) % n) + 1) for i in range(n)]
    return lax.ppermute(x, (axis, "core"), perm)


def swap(x, axis):
    return lax.ppermute(x, axis, [(0, 1), (1, 0)])


def after(x, *others):
    return lax.optimization_barrier((x, *others))[0]


def trade(parts):
    across = lax.ppermute(parts[3], ("ylo", "core"), [(0, 3), (1, 2), (2, 1), (3, 0)])
    return parts[0], swap(parts[1], "core"), swap(parts[2], "ylo"), across


def local(inputs, projected, filters, grad_out):
    count, width = grad_out.shape
    chans = filters.shape[0]
    owners = count // chans
    n = lax.axis_size("z")
    n_x = lax.axis_size("x")
    bf16 = jnp.bfloat16
    place = jnp.stack([lax.axis_index(a) for a in ("ylo", "z", "core", "x")]).astype(jnp.int32)
    rows = inputs.shape[0] // (owners * n_x)

    sent = pl.pallas_call(
        functools.partial(pack_kernel, chans),
        out_shape=jax.ShapeDtypeStruct((owners, 4 * chans + rows, width), bf16),
        in_specs=[pl.BlockSpec(memory_space=pl.ANY)] * 3,
        out_specs=pl.BlockSpec(memory_space=pltpu.VMEM),
        scratch_shapes=[pltpu.SemaphoreType.DMA((5,))],
    )(
        inputs.reshape(owners, n_x, rows, width),
        projected.reshape(3, owners, chans, width),
        grad_out.reshape(owners, chans, width),
    )
    sent = lax.all_to_all(sent, SEQ, split_axis=0, concat_axis=0, tiled=True)
    own_rows = sent[:, 4 * chans :]
    both_rows = jnp.stack([own_rows, swap(own_rows, "ylo")])

    block, filter_grad = spectral(sent, filters)
    a1 = spread(block, "z")
    turned = after(swap(block, "core"), block)
    b1 = spread(turned, "z")
    a1 = after(a1, turned)
    a2 = spread(a1, "z")
    both_rows = after(both_rows, a1)
    other_rows = swap(both_rows, "core")
    xa1 = spread(both_rows, "x")
    b1 = after(b1, a1)
    b2 = spread(b1, "z")
    other_rows = after(other_rows, b1)
    xb1 = spread(other_rows, "x")
    a2 = after(a2, b1)
    a3 = spread(a2, "z")
    b2 = after(b2, a2)
    b3 = spread(b2, "z")
    xa1 = after(xa1, b1)
    xa2 = spread(xa1, "x")
    a3 = after(a3, b2)
    a4 = spread(a3, "z")

    slots = (((0, 0), (1, 0), (1, 1), (2, 0), (2, 1)), ((3, 0), (3, 1), (4, 0)))
    first, last = (block, a1, b1, a2, b2), (a3, b3, a4)
    size = 3 * chans
    chunks = trade(vmem_call(chunk_kernel, [((size * len(first), width), bf16)] * 4, *first, place=place))
    far = [swap(after(xa1, a3), "core"), swap(after(xb1, a3), "core"), swap(after(xa2, b3), "core")]
    pieces = (both_rows, xa1, xb1, xa2, other_rows, *far)
    parts = vmem_call(
        functools.partial(product_kernel, False), [((size * len(first), width), bf16)] * 4, *pieces, *first, place=place
    )
    early = trade(parts)
    last = lax.optimization_barrier((*last, parts[0]))[:-1]
    parts = vmem_call(
        functools.partial(product_kernel, True), [((2 * size * len(last), width), bf16)] * 4, *pieces, *last, place=place
    )
    groups = (*early, *chunks, *trade(parts))
    proj_grad, weight_grad = vmem_call(
        functools.partial(finish_kernel, chans, n, slots),
        [((3, count, width), bf16), ((3, n_x * rows, count), jnp.float32)],
        *groups,
        scratch=[pltpu.VMEM((3, count, width), jnp.float32)],
        place=place,
    )
    return proj_grad, weight_grad.transpose(1, 0, 2), filter_grad


def solution(mesh):
    fine = Mesh(mesh.devices.reshape(2, 4, 2, 8, 2), ("yhi", "x", "ylo", "z", "core"))
    tp = ("yhi", "x")
    in_specs = (P(None, SEQ), P(None, tp, SEQ), P(tp + SEQ, None), P(tp, SEQ))
    out_specs = (P(None, tp, SEQ), P(SEQ, None, tp), P(tp + SEQ, None))
    return jax.shard_map(local, mesh=fine, in_specs=in_specs, out_specs=out_specs, check_vma=False)
```

```python
import functools
import math

import jax
import jax.numpy as jnp
import ml_dtypes
import numpy as np
from jax import lax
from jax.experimental import pallas as pl
from jax.experimental.pallas import tpu as pltpu
from jax.sharding import Mesh
from jax.sharding import PartitionSpec as P

SEQ = ("ylo", "z", "core")

def halves(table):
    high = table.astype(np.float32).astype(ml_dtypes.bfloat16)
    low = (table - high.astype(np.float64)).astype(np.float32).astype(ml_dtypes.bfloat16)
    return high, low


def tables(blocks, width):
    lead = 2 * blocks
    size = lead * width
    rows = -(-(blocks + 1) // 8) * 8
    k = np.arange(rows, dtype=np.float64)
    live = (k <= blocks).astype(np.float64)
    i = np.arange(blocks, dtype=np.float64)
    j = np.arange(width, dtype=np.float64)
    turn = 2.0 * math.pi * np.outer(k, i) / lead
    lead_fwd = np.concatenate([np.cos(turn) * live[:, None], -np.sin(turn) * live[:, None]], 0)
    weight = np.where((k == 0) | (k == blocks), 1.0, 2.0) * live / size
    lead_inv = np.concatenate([np.cos(turn).T * weight, -np.sin(turn).T * weight], 1)
    twist = 2.0 * math.pi * np.outer(k, j) / size
    tail = 2.0 * math.pi * np.outer(j, j) / width
    cos, sin = np.cos(tail), np.sin(tail)
    tail_fwd = np.block([[cos, -sin], [sin, cos]])
    fh, fl = halves(lead_fwd)
    ih, il = halves(lead_inv)
    th, tl = halves(tail_fwd)
    uh, ul = halves(tail_fwd.T.copy())
    return (
        np.concatenate([fh, fl, fh], 1),
        np.concatenate([ih, il, ih], 1),
        np.cos(twist).astype(np.float32),
        np.sin(twist).astype(np.float32),
        th,
        tl,
        uh,
        ul,
    )


def dot(a, b):
    return jnp.dot(a, b, preferred_element_type=jnp.float32)


def split(x):
    high = x.astype(jnp.bfloat16)
    return high, (x - high.astype(jnp.float32)).astype(jnp.bfloat16)


def kernel(
    chans, width, blocks, sent_ref, filt_ref, lf_ref, li_ref, tc_ref, ts_ref, th_ref, tl_ref, uh_ref, ul_ref, out_ref, taps_ref
):
    rows = tc_ref.shape[0]
    tc, ts = tc_ref[...], ts_ref[...]
    th, tl, uh, ul = th_ref[...], tl_ref[...], uh_ref[...], ul_ref[...]
    lf, li = lf_ref[...], li_ref[...]

    def flat(x):
        return pltpu.einshape("icj->i(cj)", x)

    def forward(high, low):
        if low is None:
            a = dot(lf[:, : 2 * blocks], jnp.concatenate([high, high], 0))
        else:
            a = dot(lf, jnp.concatenate([high, high, low], 0))
        parts = []
        for c in range(chans):
            ar = a[:rows, c * width : (c + 1) * width]
            ai = a[rows:, c * width : (c + 1) * width]
            parts.append(jnp.concatenate([ar * tc + ai * ts, ai * tc - ar * ts], 1))
        high, low = split(jnp.concatenate(parts, 0))
        x = dot(high, th) + dot(low, th) + dot(high, tl)
        return x[:, :width], x[:, width:]

    def inverse(re, im):
        high, low = split(jnp.concatenate([re, im], 1))
        b = dot(high, uh) + dot(low, uh) + dot(high, ul)
        parts = []
        for c in range(chans):
            br = b[c * rows : (c + 1) * rows, :width]
            bi = b[c * rows : (c + 1) * rows, width:]
            parts.append(jnp.concatenate([br * tc - bi * ts, br * ts + bi * tc], 0))
        high, low = split(jnp.concatenate(parts, 1))
        y = dot(li, jnp.concatenate([high, high, low], 0))
        return pltpu.einshape("i(cj)->icj", y, c=chans)

    def stream(s):
        return sent_ref[:, s * chans : (s + 1) * chans].astype(jnp.float32)

    def put(s, x):
        half = blocks // 2
        for i in range(blocks):
            at = i % half
            out_ref[i // half, s * chans : (s + 1) * chans, at * width : (at + 1) * width] = x[i].astype(jnp.bfloat16)

    gate = flat((stream(1) * stream(2)).astype(jnp.bfloat16).astype(jnp.float32)).astype(jnp.bfloat16)
    carr = flat((stream(3) * stream(0)).astype(jnp.bfloat16).astype(jnp.float32)).astype(jnp.bfloat16)
    filt = jnp.stack([filt_ref[:, i * width : (i + 1) * width] for i in range(blocks)], 0)
    fr, fi = forward(*split(flat(filt)))
    gr, gi = forward(gate, None)
    cr, ci = forward(carr, None)
    conv = inverse(fr * gr - fi * gi, fr * gi + fi * gr).astype(jnp.bfloat16).astype(jnp.float32)
    put(0, stream(3) * conv)
    back = inverse(fr * cr + fi * ci, fr * ci - fi * cr).astype(jnp.bfloat16).astype(jnp.float32)
    put(1, back * stream(2))
    put(2, back * stream(1))
    taps = inverse(cr * gr + ci * gi, ci * gr - cr * gi)
    for i in range(blocks):
        taps_ref[:, i * width : (i + 1) * width] = taps[i]


def vmem_call(body, outs, *args, scratch=(), place=None):
    specs = [pl.BlockSpec(memory_space=pltpu.VMEM)] * len(args)
    if place is not None:
        specs = [pl.BlockSpec(memory_space=pltpu.SMEM)] + specs
        args = (place,) + args
    return pl.pallas_call(
        body,
        out_shape=tuple(jax.ShapeDtypeStruct(shape, dtype) for shape, dtype in outs),
        in_specs=specs,
        out_specs=tuple(pl.BlockSpec(memory_space=pltpu.VMEM) for _ in outs),
        scratch_shapes=scratch,
        compiler_params=pltpu.CompilerParams(vmem_limit_bytes=24 * 1024 * 1024),
    )(*args)


def spectral(sent, filters):
    blocks, _, width = sent.shape
    chans = filters.shape[0]
    return vmem_call(
        functools.partial(kernel, chans, width, blocks),
        [((2, 3 * chans, blocks * width // 2), jnp.bfloat16), (filters.shape, jnp.float32)],
        sent,
        filters,
        *tables(blocks, width),
    )


def pack_kernel(chans, inputs_ref, projected_ref, grad_ref, out_ref, sems):
    copies = [
        pltpu.make_async_copy(projected_ref.at[s], out_ref.at[:, s * chans : (s + 1) * chans], sems.at[s])
        for s in range(3)
    ]
    copies.append(pltpu.make_async_copy(grad_ref, out_ref.at[:, 3 * chans : 4 * chans], sems.at[3]))
    copies.append(pltpu.make_async_copy(inputs_ref.at[:, lax.axis_index("x")], out_ref.at[:, 4 * chans :], sems.at[4]))
    for copy in copies:
        copy.start()
    for copy in copies:
        copy.wait()


def chunk(place_ref, blocks, ry, rc):
    y, z, c = place_ref[0], place_ref[1], place_ref[2]
    half = lax.rem(y + ry, 2)
    at = pl.multiple_of((2 * z + lax.rem(c + rc, 2)) * 128, 128)
    return jnp.concatenate([block[half, :, pl.ds(at, 128)] for block in blocks], 0)


def stack_kernel(*refs):
    blocks, out_ref = refs[:-1], refs[-1]
    count = out_ref.shape[1] // len(blocks)
    for k, block in enumerate(blocks):
        out_ref[:, k * count : (k + 1) * count] = block[...]


def product_kernel(place_ref, *refs):
    own, first, second, third, other, other_first, other_second, other_third = refs[:8]
    blocks, outs = refs[8:-4], refs[-4:]
    halves = [jnp.concatenate([block[h] for block in blocks], 0) for h in range(2)]
    rows, length = halves[0].shape
    _, steps, part, width = own.shape
    size = 4 * part
    for rc, pieces in enumerate(((own, first, third, other_second), (other, second, other_third, other_first))):
        total = None
        for h in range(2):
            span = range(h * steps // 2, (h + 1) * steps // 2)
            x = jnp.concatenate(
                [jnp.concatenate([ref[y, i] for i in span], 1) for y in range(2) for ref in pieces], 0
            )
            got = lax.dot_general(halves[h], x, (((1,), (1,)), ((), ())), preferred_element_type=jnp.float32)
            total = got if total is None else total + got
        for ry in range(2):
            t = total[:, ry * size : (ry + 1) * size]
            u = jnp.concatenate([t[:, :part], t[:, 3 * part :], t[:, 2 * part : 3 * part], t[:, part : 2 * part]], 1)
            out_ref = outs[2 * ry + rc]
            out_ref[:rows] = jnp.where(place_ref[2] == 0, u, t).astype(jnp.bfloat16)
            out_ref[rows:] = chunk(place_ref, blocks, ry, rc)


def finish_kernel(chans, n, slots, place_ref, *refs):
    groups, (proj_ref, weight_ref, turned_ref) = refs[:-3], refs[-3:]
    y, z, c, x = (place_ref[k] for k in range(4))
    for g, slot_list in enumerate(slots):
        rows = 3 * chans * len(slot_list)
        for near in range(4):
            ref = groups[4 * g + near]
            core = lax.rem(c + near % 2, 2)
            row_y = lax.rem(y + near // 2, 2) * 2 * n
            for m, (hops, turned) in enumerate(slot_list):
                owner = row_y + 2 * lax.rem(z + n - hops + 2 * hops * core, n) + (1 - core if turned else core)
                at = pl.multiple_of(owner * chans, chans)
                for s in range(3):
                    row = (3 * m + s) * chans
                    turned_ref[s, pl.ds(at, chans), :] = ref[row : row + chans, :].astype(jnp.float32)
                    proj_ref[s, pl.ds(at, chans), :] = ref[rows + row : rows + row + chans, :]
    n_x = 4
    part = weight_ref.shape[1] // n_x
    for s in range(3):
        rows = turned_ref[s].T
        for k in range(n_x):
            at = pl.multiple_of(lax.rem(x + k, n_x) * part, part)
            weight_ref[s, pl.ds(at, part), :] = rows[k * part : (k + 1) * part]


def spread(x, axis):
    n = lax.axis_size(axis)
    perm = [(2 * i, 2 * ((i + 1) % n)) for i in range(n)] + [(2 * i + 1, 2 * ((i + n - 1) % n) + 1) for i in range(n)]
    return lax.ppermute(x, (axis, "core"), perm)


def swap(x, axis):
    return lax.ppermute(x, axis, [(0, 1), (1, 0)])


def after(x, *others):
    return lax.optimization_barrier((x, *others))[0]


def trade(parts):
    across = lax.ppermute(parts[3], ("ylo", "core"), [(0, 3), (1, 2), (2, 1), (3, 0)])
    return parts[0], swap(parts[1], "core"), swap(parts[2], "ylo"), across


def local(inputs, projected, filters, grad_out):
    count, width = grad_out.shape
    chans = filters.shape[0]
    owners = count // chans
    n = lax.axis_size("z")
    n_x = lax.axis_size("x")
    bf16 = jnp.bfloat16
    place = jnp.stack([lax.axis_index(a) for a in ("ylo", "z", "core", "x")]).astype(jnp.int32)
    rows = inputs.shape[0] // (owners * n_x)

    sent = pl.pallas_call(
        functools.partial(pack_kernel, chans),
        out_shape=jax.ShapeDtypeStruct((owners, 4 * chans + rows, width), bf16),
        in_specs=[pl.BlockSpec(memory_space=pl.ANY)] * 3,
        out_specs=pl.BlockSpec(memory_space=pltpu.VMEM),
        scratch_shapes=[pltpu.SemaphoreType.DMA((5,))],
    )(
        inputs.reshape(owners, n_x, rows, width),
        projected.reshape(3, owners, chans, width),
        grad_out.reshape(owners, chans, width),
    )
    sent = lax.all_to_all(sent, SEQ, split_axis=0, concat_axis=0, tiled=True)
    own_rows = sent[:, 4 * chans :]
    sent, own_rows = lax.optimization_barrier((sent, own_rows))
    y_rows = swap(own_rows, "ylo")

    block, filter_grad = spectral(sent, filters)
    a1 = spread(block, "z")
    turned = swap(block, "core")
    turned = after(turned, block)
    b1 = spread(turned, "z")
    a1 = after(a1, turned)
    a2 = spread(a1, "z")
    b1 = after(b1, a1)
    b2 = spread(b1, "z")
    both_rows = jnp.stack([own_rows, after(y_rows, a1)])
    other_rows = swap(both_rows, "core")
    xa1 = spread(both_rows, "x")
    other_rows = after(other_rows, b1)
    xb1 = spread(other_rows, "x")
    a2 = after(a2, b1)
    a3 = spread(a2, "z")
    b2 = after(b2, a2)
    b3 = spread(b2, "z")
    xa1 = after(xa1, b1)
    xa2 = spread(xa1, "x")
    (first,) = vmem_call(stack_kernel, [((2, 6 * block.shape[1], block.shape[2]), bf16)], block, a1, b1, a2, b2, b3)
    a3 = after(a3, b2)
    a4 = spread(a3, "z")

    slots = (((0, 0), (1, 0), (1, 1), (2, 0), (2, 1), (3, 1)), ((3, 0), (4, 0)))
    first, last = (first,), (a3, a4)
    size = 3 * chans
    fa1 = swap(after(xa1, a3), "core")
    fb1 = swap(after(xb1, a3), "core")
    fa2 = swap(after(xa2, first), "core")
    far = [fa1, fb1, fa2]
    pieces = (both_rows, xa1, xb1, xa2, other_rows, *far)
    groups = ()
    for slot_list, blocks in zip(slots, (first, last)):
        if groups:
            blocks = lax.optimization_barrier((*blocks, groups[0]))[:-1]
        parts = vmem_call(
            product_kernel, [((2 * size * len(slot_list), width), bf16)] * 4, *pieces, *blocks, place=place
        )
        groups += trade(parts)
    proj_grad, weight_grad = vmem_call(
        functools.partial(finish_kernel, chans, n, slots),
        [((3, count, width), bf16), ((3, n_x * rows, count), jnp.float32)],
        *groups,
        scratch=[pltpu.VMEM((3, count, width), jnp.float32)],
        place=place,
    )
    return proj_grad, weight_grad.transpose(1, 0, 2), filter_grad


def solution(mesh):
    fine = Mesh(mesh.devices.reshape(2, 4, 2, 8, 2), ("yhi", "x", "ylo", "z", "core"))
    tp = ("yhi", "x")
    in_specs = (P(None, SEQ), P(None, tp, SEQ), P(tp + SEQ, None), P(tp, SEQ))
    out_specs = (P(None, tp, SEQ), P(SEQ, None, tp), P(tp + SEQ, None))
    return jax.shard_map(local, mesh=fine, in_specs=in_specs, out_specs=out_specs, check_vma=False)
```

```python
import functools
import math

import jax
import jax.numpy as jnp
import ml_dtypes
import numpy as np
from jax import lax
from jax.experimental import pallas as pl
from jax.experimental.pallas import tpu as pltpu
from jax.sharding import Mesh
from jax.sharding import PartitionSpec as P

SEQ = ("ylo", "z", "core")

def halves(table):
    high = table.astype(np.float32).astype(ml_dtypes.bfloat16)
    low = (table - high.astype(np.float64)).astype(np.float32).astype(ml_dtypes.bfloat16)
    return high, low


def tables(blocks, width):
    lead = 2 * blocks
    size = lead * width
    rows = -(-(blocks + 1) // 8) * 8
    k = np.arange(rows, dtype=np.float64)
    live = (k <= blocks).astype(np.float64)
    i = np.arange(blocks, dtype=np.float64)
    j = np.arange(width, dtype=np.float64)
    turn = 2.0 * math.pi * np.outer(k, i) / lead
    lead_fwd = np.concatenate([np.cos(turn) * live[:, None], -np.sin(turn) * live[:, None]], 0)
    weight = np.where((k == 0) | (k == blocks), 1.0, 2.0) * live / size
    lead_inv = np.concatenate([np.cos(turn).T * weight, -np.sin(turn).T * weight], 1)
    twist = 2.0 * math.pi * np.outer(k, j) / size
    tail = 2.0 * math.pi * np.outer(j, j) / width
    cos, sin = np.cos(tail), np.sin(tail)
    tail_fwd = np.block([[cos, -sin], [sin, cos]])
    fh, fl = halves(lead_fwd)
    ih, il = halves(lead_inv)
    th, tl = halves(tail_fwd)
    uh, ul = halves(tail_fwd.T.copy())
    return (
        np.concatenate([fh, fl, fh], 1),
        np.concatenate([ih, il, ih], 1),
        np.cos(twist).astype(np.float32),
        np.sin(twist).astype(np.float32),
        th,
        tl,
        uh,
        ul,
    )


def dot(a, b):
    return jnp.dot(a, b, preferred_element_type=jnp.float32)


def split(x):
    high = x.astype(jnp.bfloat16)
    return high, (x - high.astype(jnp.float32)).astype(jnp.bfloat16)


def kernel(
    chans, width, blocks, sent_ref, filt_ref, lf_ref, li_ref, tc_ref, ts_ref, th_ref, tl_ref, uh_ref, ul_ref, out_ref, taps_ref
):
    rows = tc_ref.shape[0]
    tc, ts = tc_ref[...], ts_ref[...]
    th, tl, uh, ul = th_ref[...], tl_ref[...], uh_ref[...], ul_ref[...]
    lf, li = lf_ref[...], li_ref[...]

    def flat(x):
        return pltpu.einshape("icj->i(cj)", x)

    def forward(high, low):
        if low is None:
            a = dot(lf[:, : 2 * blocks], jnp.concatenate([high, high], 0))
        else:
            a = dot(lf, jnp.concatenate([high, high, low], 0))
        parts = []
        for c in range(chans):
            ar = a[:rows, c * width : (c + 1) * width]
            ai = a[rows:, c * width : (c + 1) * width]
            parts.append(jnp.concatenate([ar * tc + ai * ts, ai * tc - ar * ts], 1))
        high, low = split(jnp.concatenate(parts, 0))
        x = dot(high, th) + dot(low, th) + dot(high, tl)
        return x[:, :width], x[:, width:]

    def inverse(re, im):
        high, low = split(jnp.concatenate([re, im], 1))
        b = dot(high, uh) + dot(low, uh) + dot(high, ul)
        parts = []
        for c in range(chans):
            br = b[c * rows : (c + 1) * rows, :width]
            bi = b[c * rows : (c + 1) * rows, width:]
            parts.append(jnp.concatenate([br * tc - bi * ts, br * ts + bi * tc], 0))
        high, low = split(jnp.concatenate(parts, 1))
        y = dot(li, jnp.concatenate([high, high, low], 0))
        return pltpu.einshape("i(cj)->icj", y, c=chans)

    def stream(s):
        return sent_ref[:, s * chans : (s + 1) * chans].astype(jnp.float32)

    def put(s, x):
        half = blocks // 2
        for i in range(blocks):
            at = i % half
            out_ref[i // half, s * chans : (s + 1) * chans, at * width : (at + 1) * width] = x[i].astype(jnp.bfloat16)

    gate = flat((stream(1) * stream(2)).astype(jnp.bfloat16).astype(jnp.float32)).astype(jnp.bfloat16)
    carr = flat((stream(3) * stream(0)).astype(jnp.bfloat16).astype(jnp.float32)).astype(jnp.bfloat16)
    filt = jnp.stack([filt_ref[:, i * width : (i + 1) * width] for i in range(blocks)], 0)
    fr, fi = forward(*split(flat(filt)))
    gr, gi = forward(gate, None)
    cr, ci = forward(carr, None)
    conv = inverse(fr * gr - fi * gi, fr * gi + fi * gr).astype(jnp.bfloat16).astype(jnp.float32)
    put(0, stream(3) * conv)
    back = inverse(fr * cr + fi * ci, fr * ci - fi * cr).astype(jnp.bfloat16).astype(jnp.float32)
    put(1, back * stream(2))
    put(2, back * stream(1))
    taps = inverse(cr * gr + ci * gi, ci * gr - cr * gi)
    for i in range(blocks):
        taps_ref[:, i * width : (i + 1) * width] = taps[i]


def vmem_call(body, outs, *args, scratch=(), place=None):
    specs = [pl.BlockSpec(memory_space=pltpu.VMEM)] * len(args)
    if place is not None:
        specs = [pl.BlockSpec(memory_space=pltpu.SMEM)] + specs
        args = (place,) + args
    return pl.pallas_call(
        body,
        out_shape=tuple(jax.ShapeDtypeStruct(shape, dtype) for shape, dtype in outs),
        in_specs=specs,
        out_specs=tuple(pl.BlockSpec(memory_space=pltpu.VMEM) for _ in outs),
        scratch_shapes=scratch,
        compiler_params=pltpu.CompilerParams(vmem_limit_bytes=24 * 1024 * 1024),
    )(*args)


def spectral(sent, filters):
    blocks, _, width = sent.shape
    chans = filters.shape[0]
    return vmem_call(
        functools.partial(kernel, chans, width, blocks),
        [((2, 3 * chans, blocks * width // 2), jnp.bfloat16), (filters.shape, jnp.float32)],
        sent,
        filters,
        *tables(blocks, width),
    )


def pack_kernel(chans, inputs_ref, projected_ref, grad_ref, out_ref, sems):
    copies = [
        pltpu.make_async_copy(projected_ref.at[s], out_ref.at[:, s * chans : (s + 1) * chans], sems.at[s])
        for s in range(3)
    ]
    copies.append(pltpu.make_async_copy(grad_ref, out_ref.at[:, 3 * chans : 4 * chans], sems.at[3]))
    copies.append(pltpu.make_async_copy(inputs_ref.at[:, lax.axis_index("x")], out_ref.at[:, 4 * chans :], sems.at[4]))
    for copy in copies:
        copy.start()
    for copy in copies:
        copy.wait()


def chunk(place_ref, blocks, ry, rc):
    y, z, c = place_ref[0], place_ref[1], place_ref[2]
    half = lax.rem(y + ry, 2)
    at = pl.multiple_of((2 * z + lax.rem(c + rc, 2)) * 128, 128)
    return jnp.concatenate([block[half, :, pl.ds(at, 128)] for block in blocks], 0)


def stack_kernel(*refs):
    blocks, out_ref = refs[:-1], refs[-1]
    count = out_ref.shape[1] // len(blocks)
    for k, block in enumerate(blocks):
        out_ref[:, k * count : (k + 1) * count] = block[...]


def product_kernel(place_ref, *refs):
    if len(refs) == 14:
        own, first, second, third, other, other_first, other_second, other_third = refs[:8]
        block, outs, x_ref = refs[8], refs[9:13], refs[13]
        _, steps, part, width = own.shape
        for rc, pieces in enumerate(((own, first, third, other_second), (other, second, other_third, other_first))):
            for ry in range(2):
                for k, ref in enumerate(pieces):
                    row = ((2 * rc + ry) * 4 + k) * part
                    for i in range(steps):
                        x_ref[row : row + part, i * width : (i + 1) * width] = ref[ry, i]
    else:
        x_ref, block, outs = refs[0], refs[1], refs[2:]
    _, rows, length = block.shape
    size = x_ref.shape[0] // 4
    part = size // 4
    for rc in range(2):
        total = None
        for h in range(2):
            x = x_ref[2 * rc * size : 2 * (rc + 1) * size, h * length : (h + 1) * length]
            got = lax.dot_general(block[h], x, (((1,), (1,)), ((), ())), preferred_element_type=jnp.float32)
            total = got if total is None else total + got
        for ry in range(2):
            t = total[:, ry * size : (ry + 1) * size]
            u = jnp.concatenate([t[:, :part], t[:, 3 * part :], t[:, 2 * part : 3 * part], t[:, part : 2 * part]], 1)
            out_ref = outs[2 * ry + rc]
            out_ref[:rows] = jnp.where(place_ref[2] == 0, u, t).astype(jnp.bfloat16)
            out_ref[rows:] = chunk(place_ref, [block], ry, rc)


def finish_kernel(chans, n, slots, place_ref, *refs):
    groups, (proj_ref, weight_ref, turned_ref) = refs[:-3], refs[-3:]
    y, z, c, x = (place_ref[k] for k in range(4))
    for g, slot_list in enumerate(slots):
        rows = 3 * chans * len(slot_list)
        for near in range(4):
            ref = groups[4 * g + near]
            core = lax.rem(c + near % 2, 2)
            row_y = lax.rem(y + near // 2, 2) * 2 * n
            for m, (hops, turned) in enumerate(slot_list):
                owner = row_y + 2 * lax.rem(z + n - hops + 2 * hops * core, n) + (1 - core if turned else core)
                at = pl.multiple_of(owner * chans, chans)
                for s in range(3):
                    row = (3 * m + s) * chans
                    turned_ref[s, pl.ds(at, chans), :] = ref[row : row + chans, :].astype(jnp.float32)
                    proj_ref[s, pl.ds(at, chans), :] = ref[rows + row : rows + row + chans, :]
    n_x = 4
    part = weight_ref.shape[1] // n_x
    for s in range(3):
        rows = turned_ref[s].T
        for k in range(n_x):
            at = pl.multiple_of(lax.rem(x + k, n_x) * part, part)
            weight_ref[s, pl.ds(at, part), :] = rows[k * part : (k + 1) * part]


def spread(x, axis, crossed=False, hops=1):
    n = lax.axis_size(axis)
    perm = []
    for i in range(n):
        for core, way in ((0, 1), (1, -1)):
            perm.append((2 * i + (1 - core if crossed else core), 2 * ((i + way * hops) % n) + core))
    return lax.ppermute(x, (axis, "core"), perm)


def swap(x, axis):
    return lax.ppermute(x, axis, [(0, 1), (1, 0)])


def after(x, *others):
    return lax.optimization_barrier((x, *others))[0]


def trade(parts):
    across = lax.ppermute(parts[3], ("ylo", "core"), [(0, 3), (1, 2), (2, 1), (3, 0)])
    return parts[0], swap(parts[1], "core"), swap(parts[2], "ylo"), across


def local(inputs, projected, filters, grad_out):
    count, width = grad_out.shape
    chans = filters.shape[0]
    owners = count // chans
    n = lax.axis_size("z")
    n_x = lax.axis_size("x")
    bf16 = jnp.bfloat16
    place = jnp.stack([lax.axis_index(a) for a in ("ylo", "z", "core", "x")]).astype(jnp.int32)
    rows = inputs.shape[0] // (owners * n_x)

    sent = pl.pallas_call(
        functools.partial(pack_kernel, chans),
        out_shape=jax.ShapeDtypeStruct((owners, 4 * chans + rows, width), bf16),
        in_specs=[pl.BlockSpec(memory_space=pl.ANY)] * 3,
        out_specs=pl.BlockSpec(memory_space=pltpu.VMEM),
        scratch_shapes=[pltpu.SemaphoreType.DMA((5,))],
    )(
        inputs.reshape(owners, n_x, rows, width),
        projected.reshape(3, owners, chans, width),
        grad_out.reshape(owners, chans, width),
    )
    sent = lax.all_to_all(sent, SEQ, split_axis=0, concat_axis=0, tiled=True)
    own_rows = sent[:, 4 * chans :]
    sent, own_rows = lax.optimization_barrier((sent, own_rows))
    y_rows = swap(own_rows, "ylo")

    block, filter_grad = spectral(sent, filters)
    a1 = spread(block, "z")
    start, y_rows = lax.optimization_barrier((block, y_rows))
    b1 = spread(start, "z", True)
    a2 = spread(after(a1, block), "z")
    b1 = after(b1, a1)
    b2 = spread(b1, "z")
    both_rows = jnp.stack([own_rows, after(y_rows, block)])
    other_rows = swap(after(both_rows, b1), "core")
    xa1 = spread(both_rows, "x")
    xb1 = spread(after(both_rows, a1), "x", True)
    a2 = after(a2, b1)
    a3 = spread(a2, "z")
    b2 = after(b2, a2)
    b3 = spread(b2, "z")
    xa1 = after(xa1, a2)
    xa2 = spread(xa1, "x")
    (first,) = vmem_call(stack_kernel, [((2, 7 * block.shape[1], block.shape[2]), bf16)], block, a1, b1, a2, b2, a3, b3)
    a3 = after(a3, b2)
    a4 = spread(a3, "z")

    slots = (((0, 0), (1, 0), (1, 1), (2, 0), (2, 1), (3, 0), (3, 1)), ((4, 0),))
    fa1 = swap(after(xa1, a3), "core")
    fb1 = swap(after(xb1, a3), "core")
    fa2 = swap(after(xa2, first), "core")
    pieces = (both_rows, xa1, xb1, xa2, other_rows, fa1, fb1, fa2)
    *parts, whole = vmem_call(
        product_kernel,
        [((2 * first.shape[1], width), bf16)] * 4 + [((4 * n_x * rows, owners * width), bf16)],
        *pieces,
        first,
        place=place,
    )
    groups = trade(parts)
    a4 = after(a4, parts[0])
    parts = vmem_call(product_kernel, [((2 * a4.shape[1], width), bf16)] * 4, whole, a4, place=place)
    groups += trade(parts)
    proj_grad, weight_grad = vmem_call(
        functools.partial(finish_kernel, chans, n, slots),
        [((3, count, width), bf16), ((3, n_x * rows, count), jnp.float32)],
        *groups,
        scratch=[pltpu.VMEM((3, count, width), jnp.float32)],
        place=place,
    )
    return proj_grad, weight_grad.transpose(1, 0, 2), filter_grad


def solution(mesh):
    fine = Mesh(mesh.devices.reshape(2, 4, 2, 8, 2), ("yhi", "x", "ylo", "z", "core"))
    tp = ("yhi", "x")
    in_specs = (P(None, SEQ), P(None, tp, SEQ), P(tp + SEQ, None), P(tp, SEQ))
    out_specs = (P(None, tp, SEQ), P(SEQ, None, tp), P(tp + SEQ, None))
    return jax.shard_map(local, mesh=fine, in_specs=in_specs, out_specs=out_specs, check_vma=False)
```

```python
import functools
import math

import jax
import jax.numpy as jnp
import ml_dtypes
import numpy as np
from jax import lax
from jax.experimental import pallas as pl
from jax.experimental.pallas import tpu as pltpu
from jax.sharding import Mesh
from jax.sharding import PartitionSpec as P

SEQ = ("ylo", "z", "core")

def halves(table):
    high = table.astype(np.float32).astype(ml_dtypes.bfloat16)
    low = (table - high.astype(np.float64)).astype(np.float32).astype(ml_dtypes.bfloat16)
    return high, low


def tables(blocks, width):
    lead = 2 * blocks
    size = lead * width
    rows = -(-(blocks + 1) // 8) * 8
    k = np.arange(rows, dtype=np.float64)
    live = (k <= blocks).astype(np.float64)
    i = np.arange(blocks, dtype=np.float64)
    j = np.arange(width, dtype=np.float64)
    turn = 2.0 * math.pi * np.outer(k, i) / lead
    lead_fwd = np.concatenate([np.cos(turn) * live[:, None], -np.sin(turn) * live[:, None]], 0)
    weight = np.where((k == 0) | (k == blocks), 1.0, 2.0) * live / size
    lead_inv = np.concatenate([np.cos(turn).T * weight, -np.sin(turn).T * weight], 1)
    twist = 2.0 * math.pi * np.outer(k, j) / size
    tail = 2.0 * math.pi * np.outer(j, j) / width
    cos, sin = np.cos(tail), np.sin(tail)
    tail_fwd = np.block([[cos, -sin], [sin, cos]])
    fh, fl = halves(lead_fwd)
    ih, il = halves(lead_inv)
    th, tl = halves(tail_fwd)
    uh, ul = halves(tail_fwd.T.copy())
    return (
        np.concatenate([fh, fl, fh], 1),
        np.concatenate([ih, il, ih], 1),
        np.cos(twist).astype(np.float32),
        np.sin(twist).astype(np.float32),
        th,
        tl,
        uh,
        ul,
    )


def dot(a, b):
    return jnp.dot(a, b, preferred_element_type=jnp.float32)


def split(x):
    high = x.astype(jnp.bfloat16)
    return high, (x - high.astype(jnp.float32)).astype(jnp.bfloat16)


def flat(x):
    return pltpu.einshape("icj->i(cj)", x)


def forward(high, low, chans, width, tables):
    lf, tc, ts, th, tl = tables
    rows = tc.shape[0]
    blocks = high.shape[0]
    if low is None:
        a = dot(lf[:, : 2 * blocks], jnp.concatenate([high, high], 0))
    else:
        a = dot(lf, jnp.concatenate([high, high, low], 0))
    parts = []
    for c in range(chans):
        ar = a[:rows, c * width : (c + 1) * width]
        ai = a[rows:, c * width : (c + 1) * width]
        parts.append(jnp.concatenate([ar * tc + ai * ts, ai * tc - ar * ts], 1))
    high, low = split(jnp.concatenate(parts, 0))
    return dot(high, th) + dot(low, th) + dot(high, tl)


def filter_kernel(chans, width, blocks, filt_ref, lf_ref, tc_ref, ts_ref, th_ref, tl_ref, out_ref):
    filt = jnp.stack([filt_ref[:, i * width : (i + 1) * width] for i in range(blocks)], 0)
    tables = tuple(ref[...] for ref in (lf_ref, tc_ref, ts_ref, th_ref, tl_ref))
    out_ref[...] = forward(*split(flat(filt)), chans, width, tables)


def kernel(
    chans, width, blocks, sent_ref, spec_ref, lf_ref, li_ref, tc_ref, ts_ref, th_ref, tl_ref, uh_ref, ul_ref, out_ref, taps_ref
):
    rows = tc_ref.shape[0]
    tc, ts = tc_ref[...], ts_ref[...]
    th, tl, uh, ul = th_ref[...], tl_ref[...], uh_ref[...], ul_ref[...]
    lf, li = lf_ref[...], li_ref[...]

    def inverse(re, im):
        high, low = split(jnp.concatenate([re, im], 1))
        b = dot(high, uh) + dot(low, uh) + dot(high, ul)
        parts = []
        for c in range(chans):
            br = b[c * rows : (c + 1) * rows, :width]
            bi = b[c * rows : (c + 1) * rows, width:]
            parts.append(jnp.concatenate([br * tc - bi * ts, br * ts + bi * tc], 0))
        high, low = split(jnp.concatenate(parts, 1))
        y = dot(li, jnp.concatenate([high, high, low], 0))
        return pltpu.einshape("i(cj)->icj", y, c=chans)

    def stream(s):
        return sent_ref[:, s * chans : (s + 1) * chans].astype(jnp.float32)

    def put(s, x):
        half = blocks // 2
        for i in range(blocks):
            at = i % half
            out_ref[i // half, s * chans : (s + 1) * chans, at * width : (at + 1) * width] = x[i].astype(jnp.bfloat16)

    gate = flat((stream(1) * stream(2)).astype(jnp.bfloat16).astype(jnp.float32)).astype(jnp.bfloat16)
    carr = flat((stream(3) * stream(0)).astype(jnp.bfloat16).astype(jnp.float32)).astype(jnp.bfloat16)
    fr, fi = spec_ref[:, :width], spec_ref[:, width:]
    gate, carr = (forward(x, None, chans, width, (lf, tc, ts, th, tl)) for x in (gate, carr))
    gr, gi = gate[:, :width], gate[:, width:]
    cr, ci = carr[:, :width], carr[:, width:]
    conv = inverse(fr * gr - fi * gi, fr * gi + fi * gr).astype(jnp.bfloat16).astype(jnp.float32)
    put(0, stream(3) * conv)
    back = inverse(fr * cr + fi * ci, fr * ci - fi * cr).astype(jnp.bfloat16).astype(jnp.float32)
    put(1, back * stream(2))
    put(2, back * stream(1))
    taps = inverse(cr * gr + ci * gi, ci * gr - cr * gi)
    for i in range(blocks):
        taps_ref[:, i * width : (i + 1) * width] = taps[i]


def vmem_call(body, outs, *args, scratch=(), place=None):
    specs = [pl.BlockSpec(memory_space=pltpu.VMEM)] * len(args)
    if place is not None:
        specs = [pl.BlockSpec(memory_space=pltpu.SMEM)] + specs
        args = (place,) + args
    return pl.pallas_call(
        body,
        out_shape=tuple(jax.ShapeDtypeStruct(shape, dtype) for shape, dtype in outs),
        in_specs=specs,
        out_specs=tuple(pl.BlockSpec(memory_space=pltpu.VMEM) for _ in outs),
        scratch_shapes=scratch,
        compiler_params=pltpu.CompilerParams(vmem_limit_bytes=24 * 1024 * 1024),
    )(*args)


def filter_spectrum(filters, blocks):
    chans, length = filters.shape
    width = length // blocks
    lf, _, tc, ts, th, tl, _, _ = tables(blocks, width)
    (spectrum,) = vmem_call(
        functools.partial(filter_kernel, chans, width, blocks),
        [((chans * tc.shape[0], 2 * width), jnp.float32)],
        filters,
        lf,
        tc,
        ts,
        th,
        tl,
    )
    return spectrum


def spectral(sent, spectrum, chans):
    blocks, _, width = sent.shape
    return vmem_call(
        functools.partial(kernel, chans, width, blocks),
        [((2, 3 * chans, blocks * width // 2), jnp.bfloat16), ((chans, blocks * width), jnp.float32)],
        sent,
        spectrum,
        *tables(blocks, width),
    )


def pack_kernel(chans, inputs_ref, projected_ref, grad_ref, out_ref, sems):
    copies = [
        pltpu.make_async_copy(projected_ref.at[s], out_ref.at[:, s * chans : (s + 1) * chans], sems.at[s])
        for s in range(3)
    ]
    copies.append(pltpu.make_async_copy(grad_ref, out_ref.at[:, 3 * chans : 4 * chans], sems.at[3]))
    copies.append(pltpu.make_async_copy(inputs_ref.at[:, lax.axis_index("x")], out_ref.at[:, 4 * chans :], sems.at[4]))
    for copy in copies:
        copy.start()
    for copy in copies:
        copy.wait()


def chunk(place_ref, blocks, ry, rc):
    y, z, c = place_ref[0], place_ref[1], place_ref[2]
    half = lax.rem(y + ry, 2)
    at = pl.multiple_of((2 * z + lax.rem(c + rc, 2)) * 128, 128)
    return jnp.concatenate([block[half, :, pl.ds(at, 128)] for block in blocks], 0)


def stack_kernel(*refs):
    blocks, out_ref = refs[:-1], refs[-1]
    count = out_ref.shape[1] // len(blocks)
    for k, block in enumerate(blocks):
        out_ref[:, k * count : (k + 1) * count] = block[...]


def chunk_kernel(place_ref, *refs):
    for near in range(4):
        refs[near - 4][...] = chunk(place_ref, refs[:-4], near // 2, near % 2)


def product_kernel(place_ref, *refs):
    if len(refs) > 10:
        own, first, second, third, other, other_first, other_second, other_third = refs[:8]
        blocks, chunked, outs, x_ref = refs[8:9], refs[9:10], refs[-5:-1], refs[-1]
        _, steps, part, width = own.shape
        for rc, pieces in enumerate(((own, first, third, other_second), (other, second, other_third, other_first))):
            for ry in range(2):
                for k, ref in enumerate(pieces):
                    row = ((2 * rc + ry) * 4 + k) * part
                    for i in range(steps):
                        x_ref[row : row + part, i * width : (i + 1) * width] = ref[ry, i]
    else:
        x_ref, blocks, outs = refs[0], refs[1:-4], refs[-4:]
        chunked = blocks
    halves = [jnp.concatenate([block[h] for block in blocks], 0) for h in range(2)]
    rows, length = halves[0].shape
    size = x_ref.shape[0] // 4
    part = size // 4
    for rc in range(2):
        total = None
        for h in range(2):
            x = x_ref[2 * rc * size : 2 * (rc + 1) * size, h * length : (h + 1) * length]
            got = lax.dot_general(halves[h], x, (((1,), (1,)), ((), ())), preferred_element_type=jnp.float32)
            total = got if total is None else total + got
        for ry in range(2):
            t = total[:, ry * size : (ry + 1) * size]
            u = jnp.concatenate([t[:, :part], t[:, 3 * part :], t[:, 2 * part : 3 * part], t[:, part : 2 * part]], 1)
            out_ref = outs[2 * ry + rc]
            out_ref[:rows] = jnp.where(place_ref[2] == 0, u, t).astype(jnp.bfloat16)
            out_ref[rows:] = chunk(place_ref, chunked, ry, rc)


def finish_kernel(chans, n, slots, place_ref, *refs):
    groups, (proj_ref, weight_ref, turned_ref) = refs[:-3], refs[-3:]
    y, z, c, x = (place_ref[k] for k in range(4))
    for near in range(4):
        core = lax.rem(c + near % 2, 2)
        row_y = lax.rem(y + near // 2, 2) * 2 * n

        def put(ref, row, slot, chunk):
            hops, turned = slot
            owner = row_y + 2 * lax.rem(z + n - hops + 2 * hops * core, n) + (1 - core if turned else core)
            at = pl.multiple_of(owner * chans, chans)
            for s in range(3):
                part = ref[row + s * chans : row + (s + 1) * chans, :]
                if chunk:
                    proj_ref[s, pl.ds(at, chans), :] = part
                else:
                    turned_ref[s, pl.ds(at, chans), :] = part.astype(jnp.float32)

        for g, (products, chunks) in enumerate(slots):
            for m, slot in enumerate(products + chunks):
                put(groups[4 * g + near], 3 * m * chans, slot, m >= len(products))
    n_x = 4
    part = weight_ref.shape[1] // n_x
    for s in range(3):
        rows = turned_ref[s].T
        for k in range(n_x):
            at = pl.multiple_of(lax.rem(x + k, n_x) * part, part)
            weight_ref[s, pl.ds(at, part), :] = rows[k * part : (k + 1) * part]


def spread(x, axis):
    n = lax.axis_size(axis)
    perm = [(2 * i, 2 * ((i + 1) % n)) for i in range(n)] + [(2 * i + 1, 2 * ((i + n - 1) % n) + 1) for i in range(n)]
    return lax.ppermute(x, (axis, "core"), perm)


def swap(x, axis):
    return lax.ppermute(x, axis, [(0, 1), (1, 0)])


def after(x, *others):
    return lax.optimization_barrier((x, *others))[0]


def trade(parts):
    across = lax.ppermute(parts[3], ("ylo", "core"), [(0, 3), (1, 2), (2, 1), (3, 0)])
    return parts[0], swap(parts[1], "core"), swap(parts[2], "ylo"), across


def local(inputs, projected, filters, grad_out):
    count, width = grad_out.shape
    chans = filters.shape[0]
    owners = count // chans
    n = lax.axis_size("z")
    n_x = lax.axis_size("x")
    bf16 = jnp.bfloat16
    place = jnp.stack([lax.axis_index(a) for a in ("ylo", "z", "core", "x")]).astype(jnp.int32)
    rows = inputs.shape[0] // (owners * n_x)

    sent = pl.pallas_call(
        functools.partial(pack_kernel, chans),
        out_shape=jax.ShapeDtypeStruct((owners, 4 * chans + rows, width), bf16),
        in_specs=[pl.BlockSpec(memory_space=pl.ANY)] * 3,
        out_specs=pl.BlockSpec(memory_space=pltpu.VMEM),
        scratch_shapes=[pltpu.SemaphoreType.DMA((5,))],
    )(
        inputs.reshape(owners, n_x, rows, width),
        projected.reshape(3, owners, chans, width),
        grad_out.reshape(owners, chans, width),
    )
    spectrum = filter_spectrum(filters, owners)
    sent = lax.all_to_all(sent, SEQ, split_axis=0, concat_axis=0, tiled=True)
    own_rows = sent[:, 4 * chans :]
    sent, own_rows = lax.optimization_barrier((sent, own_rows))
    y_rows = swap(own_rows, "ylo")

    block, filter_grad = spectral(sent, spectrum, chans)
    a1 = spread(block, "z")
    turned = swap(block, "core")
    turned = after(turned, block)
    b1 = spread(turned, "z")
    a2 = spread(after(a1, turned), "z")
    b2 = spread(after(b1, a1), "z")
    both_rows = jnp.stack([own_rows, after(y_rows, a1)])
    other_rows = swap(both_rows, "core")
    xa1 = spread(both_rows, "x")
    xb1 = spread(after(other_rows, b1), "x")
    a3 = spread(after(a2, b1), "z")
    b3 = spread(after(b2, a2), "z")
    xa2 = spread(after(xa1, b1), "x")
    (first,) = vmem_call(stack_kernel, [((2, 6 * block.shape[1], block.shape[2]), bf16)], block, a1, b1, a2, b2, b3)
    early = (block, a1, b1, a2, b2)
    chunks = trade(vmem_call(chunk_kernel, [((len(early) * block.shape[1], width), bf16)] * 4, *early, place=place))
    a4 = spread(after(a3, b2), "z")

    near_slots, last_slots = ((0, 0), (1, 0), (1, 1), (2, 0), (2, 1)), ((3, 0), (4, 0))
    slots = (((), near_slots), (near_slots + ((3, 1),), ((3, 1),)), (last_slots, last_slots))
    fa1 = swap(after(xa1, a3), "core")
    fb1 = swap(after(xb1, a3), "core")
    fa2 = swap(after(xa2, first, *chunks[1:]), "core")
    pieces = (both_rows, xa1, xb1, xa2, other_rows, fa1, fb1, fa2)
    *parts, whole = vmem_call(
        product_kernel,
        [((first.shape[1] + b3.shape[1], width), bf16)] * 4 + [((4 * n_x * rows, owners * width), bf16)],
        *pieces,
        first,
        b3,
        place=place,
    )
    groups = (*chunks, *trade(parts))
    a3, a4 = lax.optimization_barrier((a3, a4, parts[0]))[:2]
    parts = vmem_call(product_kernel, [((4 * a4.shape[1], width), bf16)] * 4, whole, a3, a4, place=place)
    groups += trade(parts)
    proj_grad, weight_grad = vmem_call(
        functools.partial(finish_kernel, chans, n, slots),
        [((3, count, width), bf16), ((3, n_x * rows, count), jnp.float32)],
        *groups,
        scratch=[pltpu.VMEM((3, count, width), jnp.float32)],
        place=place,
    )
    return proj_grad, weight_grad.transpose(1, 0, 2), filter_grad


def solution(mesh):
    fine = Mesh(mesh.devices.reshape(2, 4, 2, 8, 2), ("yhi", "x", "ylo", "z", "core"))
    tp = ("yhi", "x")
    in_specs = (P(None, SEQ), P(None, tp, SEQ), P(tp + SEQ, None), P(tp, SEQ))
    out_specs = (P(None, tp, SEQ), P(SEQ, None, tp), P(tp + SEQ, None))
    return jax.shard_map(local, mesh=fine, in_specs=in_specs, out_specs=out_specs, check_vma=False)
```

```python
import functools
import math

import jax
import jax.numpy as jnp
import ml_dtypes
import numpy as np
from jax import lax
from jax.experimental import pallas as pl
from jax.experimental.pallas import tpu as pltpu
from jax.sharding import Mesh
from jax.sharding import PartitionSpec as P

SEQ = ("ylo", "z", "core")

def halves(table):
    high = table.astype(np.float32).astype(ml_dtypes.bfloat16)
    low = (table - high.astype(np.float64)).astype(np.float32).astype(ml_dtypes.bfloat16)
    return high, low


def tables(blocks, width):
    lead = 2 * blocks
    size = lead * width
    rows = -(-(blocks + 1) // 8) * 8
    k = np.arange(rows, dtype=np.float64)
    live = (k <= blocks).astype(np.float64)
    i = np.arange(blocks, dtype=np.float64)
    j = np.arange(width, dtype=np.float64)
    turn = 2.0 * math.pi * np.outer(k, i) / lead
    lead_fwd = np.concatenate([np.cos(turn) * live[:, None], -np.sin(turn) * live[:, None]], 0)
    weight = np.where((k == 0) | (k == blocks), 1.0, 2.0) * live / size
    lead_inv = np.concatenate([np.cos(turn).T * weight, -np.sin(turn).T * weight], 1)
    twist = 2.0 * math.pi * np.outer(k, j) / size
    tail = 2.0 * math.pi * np.outer(j, j) / width
    cos, sin = np.cos(tail), np.sin(tail)
    tail_fwd = np.block([[cos, -sin], [sin, cos]])
    fh, fl = halves(lead_fwd)
    ih, il = halves(lead_inv)
    th, tl = halves(tail_fwd)
    uh, ul = halves(tail_fwd.T.copy())
    return (
        np.concatenate([fh, fl, fh], 1),
        np.concatenate([ih, il, ih], 1),
        np.cos(twist).astype(np.float32),
        np.sin(twist).astype(np.float32),
        th,
        tl,
        uh,
        ul,
    )


def dot(a, b):
    return jnp.dot(a, b, preferred_element_type=jnp.float32)


def split(x):
    high = x.astype(jnp.bfloat16)
    return high, (x - high.astype(jnp.float32)).astype(jnp.bfloat16)


def kernel(
    chans, width, blocks, sent_ref, filt_ref, lf_ref, li_ref, tc_ref, ts_ref, th_ref, tl_ref, uh_ref, ul_ref, out_ref, taps_ref, held_ref, sem
):
    rows = tc_ref.shape[0]
    tc, ts = tc_ref[...], ts_ref[...]
    th, tl, uh, ul = th_ref[...], tl_ref[...], uh_ref[...], ul_ref[...]
    lf, li = lf_ref[...], li_ref[...]

    def flat(x):
        return pltpu.einshape("icj->i(cj)", x)

    def forward(high, low):
        if low is None:
            a = dot(lf[:, : 2 * blocks], jnp.concatenate([high, high], 0))
        else:
            a = dot(lf, jnp.concatenate([high, high, low], 0))
        parts = []
        for c in range(chans):
            ar = a[:rows, c * width : (c + 1) * width]
            ai = a[rows:, c * width : (c + 1) * width]
            parts.append(jnp.concatenate([ar * tc + ai * ts, ai * tc - ar * ts], 1))
        high, low = split(jnp.concatenate(parts, 0))
        x = dot(high, th) + dot(low, th) + dot(high, tl)
        return x[:, :width], x[:, width:]

    def inverse(re, im):
        high, low = split(jnp.concatenate([re, im], 1))
        b = dot(high, uh) + dot(low, uh) + dot(high, ul)
        parts = []
        for c in range(chans):
            br = b[c * rows : (c + 1) * rows, :width]
            bi = b[c * rows : (c + 1) * rows, width:]
            parts.append(jnp.concatenate([br * tc - bi * ts, br * ts + bi * tc], 0))
        high, low = split(jnp.concatenate(parts, 1))
        y = dot(li, jnp.concatenate([high, high, low], 0))
        return pltpu.einshape("i(cj)->icj", y, c=chans)

    def stream(s):
        return sent_ref[:, s * chans : (s + 1) * chans].astype(jnp.float32)

    def put(s, x):
        half = blocks // 2
        for i in range(blocks):
            at = i % half
            out_ref[i // half, s * chans : (s + 1) * chans, at * width : (at + 1) * width] = x[i].astype(jnp.bfloat16)

    gate = flat((stream(1) * stream(2)).astype(jnp.bfloat16).astype(jnp.float32)).astype(jnp.bfloat16)
    carr = flat((stream(3) * stream(0)).astype(jnp.bfloat16).astype(jnp.float32)).astype(jnp.bfloat16)
    filt = jnp.stack([filt_ref[:, i * width : (i + 1) * width] for i in range(blocks)], 0)
    fr, fi = forward(*split(flat(filt)))
    gr, gi = forward(gate, None)
    cr, ci = forward(carr, None)
    taps = inverse(cr * gr + ci * gi, ci * gr - cr * gi)
    for i in range(blocks):
        held_ref[:, i * width : (i + 1) * width] = taps[i]
    copy = pltpu.make_async_copy(held_ref, taps_ref, sem)
    copy.start()
    conv = inverse(fr * gr - fi * gi, fr * gi + fi * gr).astype(jnp.bfloat16).astype(jnp.float32)
    put(0, stream(3) * conv)
    back = inverse(fr * cr + fi * ci, fr * ci - fi * cr).astype(jnp.bfloat16).astype(jnp.float32)
    put(1, back * stream(2))
    put(2, back * stream(1))
    copy.wait()


def vmem_call(body, outs, *args, scratch=(), place=None, away=(), micros=None):
    specs = [pl.BlockSpec(memory_space=pltpu.VMEM)] * len(args)
    if place is not None:
        specs = [pl.BlockSpec(memory_space=pltpu.SMEM)] + specs
        args = (place,) + args
    return pl.pallas_call(
        body,
        out_shape=tuple(jax.ShapeDtypeStruct(shape, dtype) for shape, dtype in outs),
        in_specs=specs,
        out_specs=tuple(pl.BlockSpec(memory_space=pl.ANY if k in away else pltpu.VMEM) for k in range(len(outs))),
        scratch_shapes=scratch,
        cost_estimate=micros
        and pl.CostEstimate(flops=int(micros * 1.15e9), bytes_accessed=int(micros * 3.6e6), transcendentals=0),
        compiler_params=pltpu.CompilerParams(vmem_limit_bytes=24 * 1024 * 1024),
    )(*args)


def spectral(sent, filters):
    blocks, _, width = sent.shape
    chans = filters.shape[0]
    return vmem_call(
        functools.partial(kernel, chans, width, blocks),
        [((2, 3 * chans, blocks * width // 2), jnp.bfloat16), (filters.shape, jnp.float32)],
        sent,
        filters,
        *tables(blocks, width),
        scratch=[pltpu.VMEM(filters.shape, jnp.float32), pltpu.SemaphoreType.DMA],
        away=(1,),
    )


def pack_kernel(chans, parts, inputs_ref, projected_ref, grad_ref, out_ref, sems):
    owners = inputs_ref.shape[0]
    step = owners // parts
    copies = []
    for k in range(parts):
        here = pl.ds(k * step, step)
        sources = [projected_ref.at[s, here] for s in range(3)] + [grad_ref.at[here]]
        sources.append(inputs_ref.at[here, lax.axis_index("x")])
        for s, source in enumerate(sources):
            rows = pl.ds(s * chans, source.shape[1])
            copies.append(pltpu.make_async_copy(source, out_ref.at[here, rows], sems.at[k, s]))
    for copy in copies:
        copy.start()
    for copy in copies:
        copy.wait()


def chunk(place_ref, blocks, ry, rc):
    y, z, c = place_ref[0], place_ref[1], place_ref[2]
    half = lax.rem(y + ry, 2)
    at = pl.multiple_of((2 * z + lax.rem(c + rc, 2)) * 128, 128)
    return jnp.concatenate([block[half, :, pl.ds(at, 128)] for block in blocks], 0)


def stack_kernel(*refs):
    blocks, out_ref = refs[:-1], refs[-1]
    count = out_ref.shape[1] // len(blocks)
    for k, block in enumerate(blocks):
        out_ref[:, k * count : (k + 1) * count] = block[...]


def product_kernel(place_ref, *refs):
    if len(refs) > 10:
        own, first, second, third, other, other_first, other_second, other_third = refs[:8]
        blocks, outs, x_ref = refs[8:-5], refs[-5:-1], refs[-1]
        _, steps, part, width = own.shape
        for rc, pieces in enumerate(((own, first, third, other_second), (other, second, other_third, other_first))):
            for ry in range(2):
                for k, ref in enumerate(pieces):
                    row = ((2 * rc + ry) * 4 + k) * part
                    for i in range(steps):
                        x_ref[row : row + part, i * width : (i + 1) * width] = ref[ry, i]
    else:
        x_ref, blocks, outs = refs[0], refs[1:-4], refs[-4:]
    halves = [jnp.concatenate([block[h] for block in blocks], 0) for h in range(2)]
    rows, length = halves[0].shape
    size = x_ref.shape[0] // 4
    part = size // 4
    for rc in range(2):
        total = None
        for h in range(2):
            x = x_ref[2 * rc * size : 2 * (rc + 1) * size, h * length : (h + 1) * length]
            got = lax.dot_general(halves[h], x, (((1,), (1,)), ((), ())), preferred_element_type=jnp.float32)
            total = got if total is None else total + got
        for ry in range(2):
            t = total[:, ry * size : (ry + 1) * size]
            u = jnp.concatenate([t[:, :part], t[:, 3 * part :], t[:, 2 * part : 3 * part], t[:, part : 2 * part]], 1)
            out_ref = outs[2 * ry + rc]
            out_ref[:rows] = jnp.where(place_ref[2] == 0, u, t).astype(jnp.bfloat16)
            out_ref[rows:] = chunk(place_ref, blocks, ry, rc)


def finish_kernel(chans, n, slots, place_ref, *refs):
    groups, (proj_out, weight_out, proj_ref, weight_ref, turned_ref, sems) = refs[:-6], refs[-6:]
    y, z, c, x = (place_ref[k] for k in range(4))
    for g, slot_list in enumerate(slots):
        rows = 3 * chans * len(slot_list)
        for near in range(4):
            ref = groups[4 * g + near]
            core = lax.rem(c + near % 2, 2)
            row_y = lax.rem(y + near // 2, 2) * 2 * n
            for m, (hops, turned) in enumerate(slot_list):
                owner = row_y + 2 * lax.rem(z + n - hops + 2 * hops * core, n) + (1 - core if turned else core)
                at = pl.multiple_of(owner * chans, chans)
                for s in range(3):
                    row = (3 * m + s) * chans
                    turned_ref[s, pl.ds(at, chans), :] = ref[row : row + chans, :].astype(jnp.float32)
                    proj_ref[s, pl.ds(at, chans), :] = ref[rows + row : rows + row + chans, :]
    copies = [pltpu.make_async_copy(proj_ref, proj_out, sems.at[3])]
    copies[0].start()
    n_x = 4
    part = weight_ref.shape[1] // n_x
    for s in range(3):
        rows = turned_ref[s].T
        for k in range(n_x):
            at = pl.multiple_of(lax.rem(x + k, n_x) * part, part)
            weight_ref[s, pl.ds(at, part), :] = rows[k * part : (k + 1) * part]
        copies.append(pltpu.make_async_copy(weight_ref.at[s], weight_out.at[s], sems.at[s]))
        copies[-1].start()
    for copy in copies:
        copy.wait()


def spread(x, axis):
    n = lax.axis_size(axis)
    perm = [(2 * i, 2 * ((i + 1) % n)) for i in range(n)] + [(2 * i + 1, 2 * ((i + n - 1) % n) + 1) for i in range(n)]
    return lax.ppermute(x, (axis, "core"), perm)


def swap(x, axis):
    return lax.ppermute(x, axis, [(0, 1), (1, 0)])


def after(x, *others):
    return lax.optimization_barrier((x, *others))[0]


def trade(parts):
    across = lax.ppermute(parts[3], ("ylo", "core"), [(0, 3), (1, 2), (2, 1), (3, 0)])
    return parts[0], swap(parts[1], "core"), swap(parts[2], "ylo"), across


def local(inputs, projected, filters, grad_out):
    count, width = grad_out.shape
    chans = filters.shape[0]
    owners = count // chans
    n = lax.axis_size("z")
    n_x = lax.axis_size("x")
    bf16 = jnp.bfloat16
    place = jnp.stack([lax.axis_index(a) for a in ("ylo", "z", "core", "x")]).astype(jnp.int32)
    rows = inputs.shape[0] // (owners * n_x)

    sent = pl.pallas_call(
        functools.partial(pack_kernel, chans, 4),
        out_shape=jax.ShapeDtypeStruct((owners, 4 * chans + rows, width), bf16),
        in_specs=[pl.BlockSpec(memory_space=pl.ANY)] * 3,
        out_specs=pl.BlockSpec(memory_space=pltpu.VMEM),
        scratch_shapes=[pltpu.SemaphoreType.DMA((4, 5))],
    )(
        inputs.reshape(owners, n_x, rows, width),
        projected.reshape(3, owners, chans, width),
        grad_out.reshape(owners, chans, width),
    )
    sent = lax.all_to_all(sent, SEQ, split_axis=0, concat_axis=0, tiled=True)
    own_rows = sent[:, 4 * chans :]
    sent, own_rows = lax.optimization_barrier((sent, own_rows))
    y_rows = swap(own_rows, "ylo")

    block, filter_grad = spectral(sent, filters)
    a1 = spread(block, "z")
    turned = swap(block, "core")
    turned = after(turned, block)
    b1 = spread(turned, "z")
    a2 = spread(after(a1, turned), "z")
    b2 = spread(after(b1, a1), "z")
    both_rows = jnp.stack([own_rows, after(y_rows, a1)])
    other_rows = swap(both_rows, "core")
    xa1 = spread(both_rows, "x")
    xb1 = spread(after(other_rows, b1), "x")
    a3 = spread(after(a2, b1), "z")
    b3 = spread(after(b2, a2), "z")
    xa2 = spread(after(xa1, b1), "x")
    (first,) = vmem_call(stack_kernel, [((2, 6 * block.shape[1], block.shape[2]), bf16)], block, a1, b1, a2, b2, b3, micros=5)
    a4 = spread(after(a3, b2), "z")

    slots = (((0, 0), (1, 0), (1, 1), (2, 0), (2, 1), (3, 1)), ((3, 0), (4, 0)))
    fa1 = swap(after(xa1, a3), "core")
    fb1 = swap(after(xb1, a3), "core")
    fa2 = swap(after(xa2, first), "core")
    pieces = (both_rows, xa1, xb1, xa2, other_rows, fa1, fb1, fa2)
    *parts, whole = vmem_call(
        product_kernel,
        [((2 * first.shape[1], width), bf16)] * 4 + [((4 * n_x * rows, owners * width), bf16)],
        *pieces,
        first,
        place=place,
    )
    groups = trade(parts)
    a3, a4 = lax.optimization_barrier((a3, a4, parts[0]))[:2]
    parts = vmem_call(product_kernel, [((4 * a4.shape[1], width), bf16)] * 4, whole, a3, a4, place=place)
    groups += trade(parts)
    proj_grad, weight_grad = vmem_call(
        functools.partial(finish_kernel, chans, n, slots),
        [((3, count, width), bf16), ((3, n_x * rows, count), jnp.float32)],
        *groups,
        scratch=[
            pltpu.VMEM((3, count, width), bf16),
            pltpu.VMEM((3, n_x * rows, count), jnp.float32),
            pltpu.VMEM((3, count, width), jnp.float32),
            pltpu.SemaphoreType.DMA((4,)),
        ],
        away=(0, 1),
        place=place,
    )
    return proj_grad, weight_grad.transpose(1, 0, 2), filter_grad


def solution(mesh):
    fine = Mesh(mesh.devices.reshape(2, 4, 2, 8, 2), ("yhi", "x", "ylo", "z", "core"))
    tp = ("yhi", "x")
    in_specs = (P(None, SEQ), P(None, tp, SEQ), P(tp + SEQ, None), P(tp, SEQ))
    out_specs = (P(None, tp, SEQ), P(SEQ, None, tp), P(tp + SEQ, None))
    return jax.shard_map(local, mesh=fine, in_specs=in_specs, out_specs=out_specs, check_vma=False)
```

```python
import functools
import math

import jax
import jax.numpy as jnp
import ml_dtypes
import numpy as np
from jax import lax
from jax.experimental import pallas as pl
from jax.experimental.pallas import tpu as pltpu
from jax.sharding import Mesh
from jax.sharding import PartitionSpec as P

SEQ = ("ylo", "z", "core")

def halves(table):
    high = table.astype(np.float32).astype(ml_dtypes.bfloat16)
    low = (table - high.astype(np.float64)).astype(np.float32).astype(ml_dtypes.bfloat16)
    return high, low


def tables(blocks, width):
    lead = 2 * blocks
    size = lead * width
    rows = -(-(blocks + 1) // 8) * 8
    k = np.arange(rows, dtype=np.float64)
    live = (k <= blocks).astype(np.float64)
    i = np.arange(blocks, dtype=np.float64)
    j = np.arange(width, dtype=np.float64)
    turn = 2.0 * math.pi * np.outer(k, i) / lead
    lead_fwd = np.concatenate([np.cos(turn) * live[:, None], -np.sin(turn) * live[:, None]], 0)
    weight = np.where((k == 0) | (k == blocks), 1.0, 2.0) * live / size
    lead_inv = np.concatenate([np.cos(turn).T * weight, -np.sin(turn).T * weight], 1)
    twist = 2.0 * math.pi * np.outer(k, j) / size
    tail = 2.0 * math.pi * np.outer(j, j) / width
    cos, sin = np.cos(tail), np.sin(tail)
    tail_fwd = np.block([[cos, -sin], [sin, cos]])
    fh, fl = halves(lead_fwd)
    ih, il = halves(lead_inv)
    th, tl = halves(tail_fwd)
    uh, ul = halves(tail_fwd.T.copy())
    return (
        np.concatenate([fh, fl, fh], 1),
        np.concatenate([ih, il, ih], 1),
        np.cos(twist).astype(np.float32),
        np.sin(twist).astype(np.float32),
        th,
        tl,
        uh,
        ul,
    )


def dot(a, b):
    return jnp.dot(a, b, preferred_element_type=jnp.float32)


def split(x):
    high = x.astype(jnp.bfloat16)
    return high, (x - high.astype(jnp.float32)).astype(jnp.bfloat16)


def kernel(
    chans, width, blocks, sent_ref, filt_ref, lf_ref, li_ref, tc_ref, ts_ref, th_ref, tl_ref, uh_ref, ul_ref, out_ref, taps_ref, held_ref, sem
):
    rows = tc_ref.shape[0]
    tc, ts = tc_ref[...], ts_ref[...]
    th, tl, uh, ul = th_ref[...], tl_ref[...], uh_ref[...], ul_ref[...]
    lf, li = lf_ref[...], li_ref[...]

    def flat(x):
        return pltpu.einshape("icj->i(cj)", x)

    def forward(high, low):
        if low is None:
            a = dot(lf[:, : 2 * blocks], jnp.concatenate([high, high], 0))
        else:
            a = dot(lf, jnp.concatenate([high, high, low], 0))
        parts = []
        for c in range(chans):
            ar = a[:rows, c * width : (c + 1) * width]
            ai = a[rows:, c * width : (c + 1) * width]
            parts.append(jnp.concatenate([ar * tc + ai * ts, ai * tc - ar * ts], 1))
        high, low = split(jnp.concatenate(parts, 0))
        x = dot(high, th) + dot(low, th) + dot(high, tl)
        return x[:, :width], x[:, width:]

    def inverse(re, im):
        high, low = split(jnp.concatenate([re, im], 1))
        b = dot(high, uh) + dot(low, uh) + dot(high, ul)
        parts = []
        for c in range(chans):
            br = b[c * rows : (c + 1) * rows, :width]
            bi = b[c * rows : (c + 1) * rows, width:]
            parts.append(jnp.concatenate([br * tc - bi * ts, br * ts + bi * tc], 0))
        high, low = split(jnp.concatenate(parts, 1))
        y = dot(li, jnp.concatenate([high, high, low], 0))
        return pltpu.einshape("i(cj)->icj", y, c=chans)

    def stream(s):
        return sent_ref[:, s * chans : (s + 1) * chans].astype(jnp.float32)

    def put(s, x):
        half = blocks // 2
        for i in range(blocks):
            at = i % half
            out_ref[i // half, s * chans : (s + 1) * chans, at * width : (at + 1) * width] = x[i].astype(jnp.bfloat16)

    gate = flat((stream(1) * stream(2)).astype(jnp.bfloat16).astype(jnp.float32)).astype(jnp.bfloat16)
    carr = flat((stream(3) * stream(0)).astype(jnp.bfloat16).astype(jnp.float32)).astype(jnp.bfloat16)
    filt = jnp.stack([filt_ref[:, i * width : (i + 1) * width] for i in range(blocks)], 0)
    fr, fi = forward(*split(flat(filt)))
    gr, gi = forward(gate, None)
    cr, ci = forward(carr, None)
    taps = inverse(cr * gr + ci * gi, ci * gr - cr * gi)
    for i in range(blocks):
        held_ref[:, i * width : (i + 1) * width] = taps[i]
    copy = pltpu.make_async_copy(held_ref, taps_ref, sem)
    copy.start()
    conv = inverse(fr * gr - fi * gi, fr * gi + fi * gr).astype(jnp.bfloat16).astype(jnp.float32)
    put(0, stream(3) * conv)
    back = inverse(fr * cr + fi * ci, fr * ci - fi * cr).astype(jnp.bfloat16).astype(jnp.float32)
    put(1, back * stream(2))
    put(2, back * stream(1))
    copy.wait()


def vmem_call(body, outs, *args, scratch=(), place=None, away=()):
    specs = [pl.BlockSpec(memory_space=pltpu.VMEM)] * len(args)
    if place is not None:
        specs = [pl.BlockSpec(memory_space=pltpu.SMEM)] + specs
        args = (place,) + args
    return pl.pallas_call(
        body,
        out_shape=tuple(jax.ShapeDtypeStruct(shape, dtype) for shape, dtype in outs),
        in_specs=specs,
        out_specs=tuple(pl.BlockSpec(memory_space=pl.ANY if k in away else pltpu.VMEM) for k in range(len(outs))),
        scratch_shapes=scratch,
        compiler_params=pltpu.CompilerParams(vmem_limit_bytes=24 * 1024 * 1024),
    )(*args)


def spectral(sent, filters):
    blocks, _, width = sent.shape
    chans = filters.shape[0]
    return vmem_call(
        functools.partial(kernel, chans, width, blocks),
        [((2, 3 * chans, blocks * width // 2), jnp.bfloat16), (filters.shape, jnp.float32)],
        sent,
        filters,
        *tables(blocks, width),
        scratch=[pltpu.VMEM(filters.shape, jnp.float32), pltpu.SemaphoreType.DMA],
        away=(1,),
    )


def pack_kernel(chans, inputs_ref, projected_ref, grad_ref, out_ref, sems):
    copies = [
        pltpu.make_async_copy(projected_ref.at[s], out_ref.at[:, s * chans : (s + 1) * chans], sems.at[s])
        for s in range(3)
    ]
    copies.append(pltpu.make_async_copy(grad_ref, out_ref.at[:, 3 * chans : 4 * chans], sems.at[3]))
    copies.append(pltpu.make_async_copy(inputs_ref.at[:, lax.axis_index("x")], out_ref.at[:, 4 * chans :], sems.at[4]))
    for copy in copies:
        copy.start()
    for copy in copies:
        copy.wait()


def chunk(place_ref, blocks, ry, rc):
    y, z, c = place_ref[0], place_ref[1], place_ref[2]
    half = lax.rem(y + ry, 2)
    at = pl.multiple_of((2 * z + lax.rem(c + rc, 2)) * 128, 128)
    return jnp.concatenate([block[half, :, pl.ds(at, 128)] for block in blocks], 0)


def stack_kernel(*refs):
    blocks, out_ref = refs[:-1], refs[-1]
    count = out_ref.shape[1] // len(blocks)
    for k, block in enumerate(blocks):
        out_ref[:, k * count : (k + 1) * count] = block[...]


def product_kernel(place_ref, *refs):
    if len(refs) > 10:
        own, first, second, third, other, other_first, other_second, other_third = refs[:8]
        blocks, outs, x_ref = refs[8:-5], refs[-5:-1], refs[-1]
        _, steps, part, width = own.shape
        for rc, pieces in enumerate(((own, first, third, other_second), (other, second, other_third, other_first))):
            for ry in range(2):
                for k, ref in enumerate(pieces):
                    row = ((2 * rc + ry) * 4 + k) * part
                    for i in range(steps):
                        x_ref[row : row + part, i * width : (i + 1) * width] = ref[ry, i]
    else:
        x_ref, blocks, outs = refs[0], refs[1:-4], refs[-4:]
    halves = [jnp.concatenate([block[h] for block in blocks], 0) for h in range(2)]
    rows, length = halves[0].shape
    size = x_ref.shape[0] // 4
    part = size // 4
    for rc in range(2):
        total = None
        for h in range(2):
            x = x_ref[2 * rc * size : 2 * (rc + 1) * size, h * length : (h + 1) * length]
            got = lax.dot_general(halves[h], x, (((1,), (1,)), ((), ())), preferred_element_type=jnp.float32)
            total = got if total is None else total + got
        for ry in range(2):
            t = total[:, ry * size : (ry + 1) * size]
            u = jnp.concatenate([t[:, :part], t[:, 3 * part :], t[:, 2 * part : 3 * part], t[:, part : 2 * part]], 1)
            out_ref = outs[2 * ry + rc]
            out_ref[:rows] = jnp.where(place_ref[2] == 0, u, t).astype(jnp.bfloat16)
            out_ref[rows:] = chunk(place_ref, blocks, ry, rc)


def finish_kernel(chans, n, slots, place_ref, *refs):
    groups, (proj_out, weight_out, proj_ref, weight_ref, turned_ref, sems) = refs[:-6], refs[-6:]
    y, z, c, x = (place_ref[k] for k in range(4))
    for g, slot_list in enumerate(slots):
        rows = 3 * chans * len(slot_list)
        for near in range(4):
            ref = groups[4 * g + near]
            core = lax.rem(c + near % 2, 2)
            row_y = lax.rem(y + near // 2, 2) * 2 * n
            for m, (hops, turned) in enumerate(slot_list):
                owner = row_y + 2 * lax.rem(z + n - hops + 2 * hops * core, n) + (1 - core if turned else core)
                at = pl.multiple_of(owner * chans, chans)
                for s in range(3):
                    row = (3 * m + s) * chans
                    turned_ref[s, pl.ds(at, chans), :] = ref[row : row + chans, :].astype(jnp.float32)
                    proj_ref[s, pl.ds(at, chans), :] = ref[rows + row : rows + row + chans, :]
    copies = [pltpu.make_async_copy(proj_ref, proj_out, sems.at[3])]
    copies[0].start()
    n_x = 4
    part = weight_ref.shape[1] // n_x
    for s in range(3):
        rows = turned_ref[s].T
        for k in range(n_x):
            at = pl.multiple_of(lax.rem(x + k, n_x) * part, part)
            weight_ref[s, pl.ds(at, part), :] = rows[k * part : (k + 1) * part]
        copies.append(pltpu.make_async_copy(weight_ref.at[s], weight_out.at[s], sems.at[s]))
        copies[-1].start()
    for copy in copies:
        copy.wait()


def spread(x, axis):
    n = lax.axis_size(axis)
    perm = [(2 * i, 2 * ((i + 1) % n)) for i in range(n)] + [(2 * i + 1, 2 * ((i + n - 1) % n) + 1) for i in range(n)]
    return lax.ppermute(x, (axis, "core"), perm)


def swap(x, axis):
    return lax.ppermute(x, axis, [(0, 1), (1, 0)])


def after(x, *others):
    return lax.optimization_barrier((x, *others))[0]


def trade(parts):
    across = lax.ppermute(parts[3], ("ylo", "core"), [(0, 3), (1, 2), (2, 1), (3, 0)])
    return parts[0], swap(parts[1], "core"), swap(parts[2], "ylo"), across


def local(inputs, projected, filters, grad_out):
    count, width = grad_out.shape
    chans = filters.shape[0]
    owners = count // chans
    n = lax.axis_size("z")
    n_x = lax.axis_size("x")
    bf16 = jnp.bfloat16
    place = jnp.stack([lax.axis_index(a) for a in ("ylo", "z", "core", "x")]).astype(jnp.int32)
    rows = inputs.shape[0] // (owners * n_x)

    sent = pl.pallas_call(
        functools.partial(pack_kernel, chans),
        out_shape=jax.ShapeDtypeStruct((owners, 4 * chans + rows, width), bf16),
        in_specs=[pl.BlockSpec(memory_space=pl.ANY)] * 3,
        out_specs=pl.BlockSpec(memory_space=pltpu.VMEM),
        scratch_shapes=[pltpu.SemaphoreType.DMA((5,))],
    )(
        inputs.reshape(owners, n_x, rows, width),
        projected.reshape(3, owners, chans, width),
        grad_out.reshape(owners, chans, width),
    )
    sent = lax.all_to_all(sent, SEQ, split_axis=0, concat_axis=0, tiled=True)
    own_rows = sent[:, 4 * chans :]
    sent, own_rows = lax.optimization_barrier((sent, own_rows))
    y_rows = swap(own_rows, "ylo")

    block, filter_grad = spectral(sent, filters)
    a1 = spread(block, "z")
    turned = swap(block, "core")
    turned = after(turned, block)
    b1 = spread(turned, "z")
    a2 = spread(after(a1, turned), "z")
    b2 = spread(after(b1, a1), "z")
    both_rows = jnp.stack([own_rows, after(y_rows, a1)])
    other_rows = swap(both_rows, "core")
    xa1 = spread(both_rows, "x")
    xb1 = spread(after(other_rows, b1), "x")
    a3 = spread(after(a2, b1), "z")
    b3 = spread(after(b2, a2), "z")
    xa2 = spread(after(xa1, b1), "x")
    (first,) = vmem_call(stack_kernel, [((2, 6 * block.shape[1], block.shape[2]), bf16)], block, a1, b1, a2, b2, b3)
    a4 = spread(after(a3, b2), "z")

    slots = (((0, 0), (1, 0), (1, 1), (2, 0), (2, 1), (3, 1)), ((3, 0), (4, 0)))
    fa1 = swap(after(xa1, a3), "core")
    fb1 = swap(after(xb1, a3), "core")
    fa2 = swap(after(xa2, first), "core")
    pieces = (both_rows, xa1, xb1, xa2, other_rows, fa1, fb1, fa2)
    *parts, whole = vmem_call(
        product_kernel,
        [((2 * first.shape[1], width), bf16)] * 4 + [((4 * n_x * rows, owners * width), bf16)],
        *pieces,
        first,
        place=place,
    )
    groups = trade(parts)
    a3, a4 = lax.optimization_barrier((a3, a4, parts[0]))[:2]
    parts = vmem_call(product_kernel, [((4 * a4.shape[1], width), bf16)] * 4, whole, a3, a4, place=place)
    groups += trade(parts)
    proj_grad, weight_grad = vmem_call(
        functools.partial(finish_kernel, chans, n, slots),
        [((3, count, width), bf16), ((3, n_x * rows, count), jnp.float32)],
        *groups,
        scratch=[
            pltpu.VMEM((3, count, width), bf16),
            pltpu.VMEM((3, n_x * rows, count), jnp.float32),
            pltpu.VMEM((3, count, width), jnp.float32),
            pltpu.SemaphoreType.DMA((4,)),
        ],
        away=(0, 1),
        place=place,
    )
    return proj_grad, weight_grad.transpose(1, 0, 2), filter_grad


def solution(mesh):
    fine = Mesh(mesh.devices.reshape(2, 4, 2, 8, 2), ("yhi", "x", "ylo", "z", "core"))
    tp = ("yhi", "x")
    in_specs = (P(None, SEQ), P(None, tp, SEQ), P(tp + SEQ, None), P(tp, SEQ))
    out_specs = (P(None, tp, SEQ), P(SEQ, None, tp), P(tp + SEQ, None))
    return jax.shard_map(local, mesh=fine, in_specs=in_specs, out_specs=out_specs, check_vma=False)
```

```python
import functools
import math

import jax
import jax.numpy as jnp
import ml_dtypes
import numpy as np
from jax import lax
from jax.experimental import pallas as pl
from jax.experimental.pallas import tpu as pltpu
from jax.sharding import Mesh
from jax.sharding import PartitionSpec as P

SEQ = ("ylo", "z", "core")

def halves(table):
    high = table.astype(np.float32).astype(ml_dtypes.bfloat16)
    low = (table - high.astype(np.float64)).astype(np.float32).astype(ml_dtypes.bfloat16)
    return high, low


def tables(blocks, width):
    lead = 2 * blocks
    size = lead * width
    rows = -(-(blocks + 1) // 8) * 8
    k = np.arange(rows, dtype=np.float64)
    live = (k <= blocks).astype(np.float64)
    i = np.arange(blocks, dtype=np.float64)
    j = np.arange(width, dtype=np.float64)
    turn = 2.0 * math.pi * np.outer(k, i) / lead
    lead_fwd = np.concatenate([np.cos(turn) * live[:, None], -np.sin(turn) * live[:, None]], 0)
    weight = np.where((k == 0) | (k == blocks), 1.0, 2.0) * live / size
    lead_inv = np.concatenate([np.cos(turn).T * weight, -np.sin(turn).T * weight], 1)
    twist = 2.0 * math.pi * np.outer(k, j) / size
    tail = 2.0 * math.pi * np.outer(j, j) / width
    cos, sin = np.cos(tail), np.sin(tail)
    tail_fwd = np.block([[cos, -sin], [sin, cos]])
    fh, fl = halves(lead_fwd)
    ih, il = halves(lead_inv)
    th, tl = halves(tail_fwd)
    uh, ul = halves(tail_fwd.T.copy())
    return (
        np.concatenate([fh, fl, fh], 1),
        np.concatenate([ih, il, ih], 1),
        np.cos(twist).astype(np.float32),
        np.sin(twist).astype(np.float32),
        th,
        tl,
        uh,
        ul,
    )


def dot(a, b):
    return jnp.dot(a, b, preferred_element_type=jnp.float32)


def split(x):
    high = x.astype(jnp.bfloat16)
    return high, (x - high.astype(jnp.float32)).astype(jnp.bfloat16)


def kernel(
    chans, width, blocks, sent_ref, filt_ref, lf_ref, li_ref, tc_ref, ts_ref, th_ref, tl_ref, uh_ref, ul_ref, out_ref, taps_ref, held_ref, sem
):
    rows = tc_ref.shape[0]
    tc, ts = tc_ref[...], ts_ref[...]
    th, tl, uh, ul = th_ref[...], tl_ref[...], uh_ref[...], ul_ref[...]
    lf, li = lf_ref[...], li_ref[...]

    def flat(x):
        return pltpu.einshape("icj->i(cj)", x)

    def forward(high, low):
        if low is None:
            a = dot(lf[:, : 2 * blocks], jnp.concatenate([high, high], 0))
        else:
            a = dot(lf, jnp.concatenate([high, high, low], 0))
        parts = []
        for c in range(chans):
            ar = a[:rows, c * width : (c + 1) * width]
            ai = a[rows:, c * width : (c + 1) * width]
            parts.append(jnp.concatenate([ar * tc + ai * ts, ai * tc - ar * ts], 1))
        high, low = split(jnp.concatenate(parts, 0))
        x = dot(high, th) + dot(low, th) + dot(high, tl)
        return x[:, :width], x[:, width:]

    def inverse(re, im):
        high, low = split(jnp.concatenate([re, im], 1))
        b = dot(high, uh) + dot(low, uh) + dot(high, ul)
        parts = []
        for c in range(chans):
            br = b[c * rows : (c + 1) * rows, :width]
            bi = b[c * rows : (c + 1) * rows, width:]
            parts.append(jnp.concatenate([br * tc - bi * ts, br * ts + bi * tc], 0))
        high, low = split(jnp.concatenate(parts, 1))
        y = dot(li, jnp.concatenate([high, high, low], 0))
        return pltpu.einshape("i(cj)->icj", y, c=chans)

    def stream(s):
        return sent_ref[:, s * chans : (s + 1) * chans].astype(jnp.float32)

    def put(s, x):
        half = blocks // 2
        for i in range(blocks):
            at = i % half
            out_ref[i // half, s * chans : (s + 1) * chans, at * width : (at + 1) * width] = x[i].astype(jnp.bfloat16)

    gate = flat((stream(1) * stream(2)).astype(jnp.bfloat16).astype(jnp.float32)).astype(jnp.bfloat16)
    carr = flat((stream(3) * stream(0)).astype(jnp.bfloat16).astype(jnp.float32)).astype(jnp.bfloat16)
    filt = jnp.stack([filt_ref[:, i * width : (i + 1) * width] for i in range(blocks)], 0)
    fr, fi = forward(*split(flat(filt)))
    gr, gi = forward(gate, None)
    cr, ci = forward(carr, None)
    taps = inverse(cr * gr + ci * gi, ci * gr - cr * gi)
    for i in range(blocks):
        held_ref[:, i * width : (i + 1) * width] = taps[i]
    copy = pltpu.make_async_copy(held_ref, taps_ref, sem)
    copy.start()
    conv = inverse(fr * gr - fi * gi, fr * gi + fi * gr).astype(jnp.bfloat16).astype(jnp.float32)
    put(0, stream(3) * conv)
    back = inverse(fr * cr + fi * ci, fr * ci - fi * cr).astype(jnp.bfloat16).astype(jnp.float32)
    put(1, back * stream(2))
    put(2, back * stream(1))
    copy.wait()


def vmem_call(body, outs, *args, scratch=(), place=None, away=()):
    specs = [pl.BlockSpec(memory_space=pltpu.VMEM)] * len(args)
    if place is not None:
        specs = [pl.BlockSpec(memory_space=pltpu.SMEM)] + specs
        args = (place,) + args
    return pl.pallas_call(
        body,
        out_shape=tuple(jax.ShapeDtypeStruct(shape, dtype) for shape, dtype in outs),
        in_specs=specs,
        out_specs=tuple(pl.BlockSpec(memory_space=pl.ANY if k in away else pltpu.VMEM) for k in range(len(outs))),
        scratch_shapes=scratch,
        compiler_params=pltpu.CompilerParams(vmem_limit_bytes=24 * 1024 * 1024),
    )(*args)


def spectral(sent, filters):
    blocks, _, width = sent.shape
    chans = filters.shape[0]
    return vmem_call(
        functools.partial(kernel, chans, width, blocks),
        [((2, 3 * chans, blocks * width // 2), jnp.bfloat16), (filters.shape, jnp.float32)],
        sent,
        filters,
        *tables(blocks, width),
        scratch=[pltpu.VMEM(filters.shape, jnp.float32), pltpu.SemaphoreType.DMA],
        away=(1,),
    )


def pack_kernel(chans, inputs_ref, projected_ref, grad_ref, out_ref, sems):
    copies = [
        pltpu.make_async_copy(projected_ref.at[s], out_ref.at[:, s * chans : (s + 1) * chans], sems.at[s])
        for s in range(3)
    ]
    copies.append(pltpu.make_async_copy(grad_ref, out_ref.at[:, 3 * chans : 4 * chans], sems.at[3]))
    copies.append(pltpu.make_async_copy(inputs_ref.at[:, lax.axis_index("x")], out_ref.at[:, 4 * chans :], sems.at[4]))
    for copy in copies:
        copy.start()
    for copy in copies:
        copy.wait()


def chunk(place_ref, blocks, ry, rc):
    y, z, c = place_ref[0], place_ref[1], place_ref[2]
    half = lax.rem(y + ry, 2)
    at = pl.multiple_of((2 * z + lax.rem(c + rc, 2)) * 128, 128)
    return jnp.concatenate([block[half, :, pl.ds(at, 128)] for block in blocks], 0)


def stack_kernel(*refs):
    blocks, out_ref = refs[:-1], refs[-1]
    count = out_ref.shape[1] // len(blocks)
    for k, block in enumerate(blocks):
        out_ref[:, k * count : (k + 1) * count] = block[...]


def product_kernel(place_ref, *refs):
    if len(refs) > 10:
        own, first, second, third, other, other_first, other_second, other_third = refs[:8]
        blocks, outs, x_ref = refs[8:-5], refs[-5:-1], refs[-1]
        _, steps, part, width = own.shape
        for rc, pieces in enumerate(((own, first, third, other_second), (other, second, other_third, other_first))):
            for ry in range(2):
                for k, ref in enumerate(pieces):
                    row = ((2 * rc + ry) * 4 + k) * part
                    for i in range(steps):
                        x_ref[row : row + part, i * width : (i + 1) * width] = ref[ry, i]
    else:
        x_ref, blocks, outs = refs[0], refs[1:-4], refs[-4:]
    halves = [jnp.concatenate([block[h] for block in blocks], 0) for h in range(2)]
    rows, length = halves[0].shape
    size = x_ref.shape[0] // 4
    part = size // 4
    for rc in range(2):
        total = None
        for h in range(2):
            x = x_ref[2 * rc * size : 2 * (rc + 1) * size, h * length : (h + 1) * length]
            got = lax.dot_general(halves[h], x, (((1,), (1,)), ((), ())), preferred_element_type=jnp.float32)
            total = got if total is None else total + got
        for ry in range(2):
            t = total[:, ry * size : (ry + 1) * size]
            u = jnp.concatenate([t[:, :part], t[:, 3 * part :], t[:, 2 * part : 3 * part], t[:, part : 2 * part]], 1)
            out_ref = outs[2 * ry + rc]
            out_ref[:rows] = jnp.where(place_ref[2] == 0, u, t).astype(jnp.bfloat16)
            out_ref[rows:] = chunk(place_ref, blocks, ry, rc)


def finish_kernel(chans, n, slots, place_ref, *refs):
    groups, (proj_out, weight_out, proj_ref, weight_ref, turned_ref, sems) = refs[:-6], refs[-6:]
    y, z, c, x = (place_ref[k] for k in range(4))
    for g, slot_list in enumerate(slots):
        rows = 3 * chans * len(slot_list)
        for near in range(4):
            ref = groups[4 * g + near]
            core = lax.rem(c + near % 2, 2)
            row_y = lax.rem(y + near // 2, 2) * 2 * n
            for m, (hops, turned) in enumerate(slot_list):
                owner = row_y + 2 * lax.rem(z + n - hops + 2 * hops * core, n) + (1 - core if turned else core)
                at = pl.multiple_of(owner * chans, chans)
                for s in range(3):
                    row = (3 * m + s) * chans
                    turned_ref[s, pl.ds(at, chans), :] = ref[row : row + chans, :].astype(jnp.float32)
                    proj_ref[s, pl.ds(at, chans), :] = ref[rows + row : rows + row + chans, :]
    copies = [pltpu.make_async_copy(proj_ref, proj_out, sems.at[3])]
    copies[0].start()
    n_x = 4
    part = weight_ref.shape[1] // n_x
    for s in range(3):
        rows = turned_ref[s].T
        for k in range(n_x):
            at = pl.multiple_of(lax.rem(x + k, n_x) * part, part)
            weight_ref[s, pl.ds(at, part), :] = rows[k * part : (k + 1) * part]
        copies.append(pltpu.make_async_copy(weight_ref.at[s], weight_out.at[s], sems.at[s]))
        copies[-1].start()
    for copy in copies:
        copy.wait()


def spread(x, axis):
    n = lax.axis_size(axis)
    perm = [(2 * i, 2 * ((i + 1) % n)) for i in range(n)] + [(2 * i + 1, 2 * ((i + n - 1) % n) + 1) for i in range(n)]
    return lax.ppermute(x, (axis, "core"), perm)


def swap(x, axis):
    return lax.ppermute(x, axis, [(0, 1), (1, 0)])


def after(x, *others):
    return lax.optimization_barrier((x, *others))[0]


def trade(parts):
    across = lax.ppermute(parts[3], ("ylo", "core"), [(0, 3), (1, 2), (2, 1), (3, 0)])
    return parts[0], swap(parts[1], "core"), swap(parts[2], "ylo"), across


def local(inputs, projected, filters, grad_out):
    count, width = grad_out.shape
    chans = filters.shape[0]
    owners = count // chans
    n = lax.axis_size("z")
    n_x = lax.axis_size("x")
    bf16 = jnp.bfloat16
    place = jnp.stack([lax.axis_index(a) for a in ("ylo", "z", "core", "x")]).astype(jnp.int32)
    rows = inputs.shape[0] // (owners * n_x)

    sent = pl.pallas_call(
        functools.partial(pack_kernel, chans),
        out_shape=jax.ShapeDtypeStruct((owners, 4 * chans + rows, width), bf16),
        in_specs=[pl.BlockSpec(memory_space=pl.ANY)] * 3,
        out_specs=pl.BlockSpec(memory_space=pltpu.VMEM),
        scratch_shapes=[pltpu.SemaphoreType.DMA((5,))],
    )(
        inputs.reshape(owners, n_x, rows, width),
        projected.reshape(3, owners, chans, width),
        grad_out.reshape(owners, chans, width),
    )
    sent = lax.all_to_all(sent, SEQ, split_axis=0, concat_axis=0, tiled=True)
    own_rows = sent[:, 4 * chans :]
    sent, own_rows = lax.optimization_barrier((sent, own_rows))
    y_rows = swap(own_rows, "ylo")

    block, filter_grad = spectral(sent, filters)
    a1 = spread(block, "z")
    start, y_rows = lax.optimization_barrier((block, y_rows))
    turned = swap(start, "core")
    b1 = spread(turned, "z")
    a2 = spread(after(a1, turned), "z")
    b2 = spread(after(b1, a1), "z")
    both_rows = jnp.stack([own_rows, after(y_rows, block)])
    other_rows = swap(both_rows, "core")
    xa1 = spread(both_rows, "x")
    xb1 = spread(after(other_rows, b1), "x")
    a3 = spread(after(a2, b1), "z")
    b3 = spread(after(b2, a2), "z")
    xa2 = spread(after(xa1, b1), "x")
    (first,) = vmem_call(stack_kernel, [((2, 6 * block.shape[1], block.shape[2]), bf16)], block, a1, b1, a2, b2, b3)
    a4 = spread(after(a3, b2), "z")

    slots = (((0, 0), (1, 0), (1, 1), (2, 0), (2, 1), (3, 1)), ((3, 0), (4, 0)))
    fa1 = swap(after(xa1, a3), "core")
    fb1 = swap(after(xb1, a3), "core")
    fa2 = swap(after(xa2, first), "core")
    pieces = (both_rows, xa1, xb1, xa2, other_rows, fa1, fb1, fa2)
    *parts, whole = vmem_call(
        product_kernel,
        [((2 * first.shape[1], width), bf16)] * 4 + [((4 * n_x * rows, owners * width), bf16)],
        *pieces,
        first,
        place=place,
    )
    groups = trade(parts)
    a3, a4 = lax.optimization_barrier((a3, a4, parts[0]))[:2]
    parts = vmem_call(product_kernel, [((4 * a4.shape[1], width), bf16)] * 4, whole, a3, a4, place=place)
    groups += trade(parts)
    proj_grad, weight_grad = vmem_call(
        functools.partial(finish_kernel, chans, n, slots),
        [((3, count, width), bf16), ((3, n_x * rows, count), jnp.float32)],
        *groups,
        scratch=[
            pltpu.VMEM((3, count, width), bf16),
            pltpu.VMEM((3, n_x * rows, count), jnp.float32),
            pltpu.VMEM((3, count, width), jnp.float32),
            pltpu.SemaphoreType.DMA((4,)),
        ],
        away=(0, 1),
        place=place,
    )
    return proj_grad, weight_grad.transpose(1, 0, 2), filter_grad


def solution(mesh):
    fine = Mesh(mesh.devices.reshape(2, 4, 2, 8, 2), ("yhi", "x", "ylo", "z", "core"))
    tp = ("yhi", "x")
    in_specs = (P(None, SEQ), P(None, tp, SEQ), P(tp + SEQ, None), P(tp, SEQ))
    out_specs = (P(None, tp, SEQ), P(SEQ, None, tp), P(tp + SEQ, None))
    return jax.shard_map(local, mesh=fine, in_specs=in_specs, out_specs=out_specs, check_vma=False)
```

```python
import functools
import math

import jax
import jax.numpy as jnp
import ml_dtypes
import numpy as np
from jax import lax
from jax.experimental import pallas as pl
from jax.experimental.pallas import tpu as pltpu
from jax.sharding import Mesh
from jax.sharding import PartitionSpec as P

SEQ = ("ylo", "z", "core")

def halves(table):
    high = table.astype(np.float32).astype(ml_dtypes.bfloat16)
    low = (table - high.astype(np.float64)).astype(np.float32).astype(ml_dtypes.bfloat16)
    return high, low


def tables(blocks, width):
    lead = 2 * blocks
    size = lead * width
    rows = -(-(blocks + 1) // 8) * 8
    k = np.arange(rows, dtype=np.float64)
    live = (k <= blocks).astype(np.float64)
    i = np.arange(blocks, dtype=np.float64)
    j = np.arange(width, dtype=np.float64)
    turn = 2.0 * math.pi * np.outer(k, i) / lead
    lead_fwd = np.concatenate([np.cos(turn) * live[:, None], -np.sin(turn) * live[:, None]], 0)
    weight = np.where((k == 0) | (k == blocks), 1.0, 2.0) * live / size
    lead_inv = np.concatenate([np.cos(turn).T * weight, -np.sin(turn).T * weight], 1)
    twist = 2.0 * math.pi * np.outer(k, j) / size
    tail = 2.0 * math.pi * np.outer(j, j) / width
    cos, sin = np.cos(tail), np.sin(tail)
    tail_fwd = np.block([[cos, -sin], [sin, cos]])
    fh, fl = halves(lead_fwd)
    ih, il = halves(lead_inv)
    th, tl = halves(tail_fwd)
    uh, ul = halves(tail_fwd.T.copy())
    return (
        np.concatenate([fh, fl, fh], 1),
        np.concatenate([ih, il, ih], 1),
        np.cos(twist).astype(np.float32),
        np.sin(twist).astype(np.float32),
        th,
        tl,
        uh,
        ul,
    )


def dot(a, b):
    return jnp.dot(a, b, preferred_element_type=jnp.float32)


def split(x):
    high = x.astype(jnp.bfloat16)
    return high, (x - high.astype(jnp.float32)).astype(jnp.bfloat16)


def inverse(re, im, chans, width, tables):
    li, tc, ts, uh, ul = tables
    rows = tc.shape[0]
    high, low = split(jnp.concatenate([re, im], 1))
    b = dot(high, uh) + dot(low, uh) + dot(high, ul)
    parts = []
    for c in range(chans):
        br = b[c * rows : (c + 1) * rows, :width]
        bi = b[c * rows : (c + 1) * rows, width:]
        parts.append(jnp.concatenate([br * tc - bi * ts, br * ts + bi * tc], 0))
    high, low = split(jnp.concatenate(parts, 1))
    y = dot(li, jnp.concatenate([high, high, low], 0))
    return pltpu.einshape("i(cj)->icj", y, c=chans)


def taps_kernel(chans, width, blocks, gate_ref, carr_ref, li_ref, tc_ref, ts_ref, uh_ref, ul_ref, taps_ref):
    gr, gi = gate_ref[:, :width], gate_ref[:, width:]
    cr, ci = carr_ref[:, :width], carr_ref[:, width:]
    tables = tuple(ref[...] for ref in (li_ref, tc_ref, ts_ref, uh_ref, ul_ref))
    taps = inverse(cr * gr + ci * gi, ci * gr - cr * gi, chans, width, tables)
    for i in range(blocks):
        taps_ref[:, i * width : (i + 1) * width] = taps[i]


def kernel(
    chans, width, blocks, sent_ref, filt_ref, lf_ref, li_ref, tc_ref, ts_ref, th_ref, tl_ref, uh_ref, ul_ref, out_ref, gate_ref, carr_ref
):
    rows = tc_ref.shape[0]
    tc, ts = tc_ref[...], ts_ref[...]
    th, tl, uh, ul = th_ref[...], tl_ref[...], uh_ref[...], ul_ref[...]
    lf, li = lf_ref[...], li_ref[...]

    def flat(x):
        return pltpu.einshape("icj->i(cj)", x)

    def forward(high, low):
        if low is None:
            a = dot(lf[:, : 2 * blocks], jnp.concatenate([high, high], 0))
        else:
            a = dot(lf, jnp.concatenate([high, high, low], 0))
        parts = []
        for c in range(chans):
            ar = a[:rows, c * width : (c + 1) * width]
            ai = a[rows:, c * width : (c + 1) * width]
            parts.append(jnp.concatenate([ar * tc + ai * ts, ai * tc - ar * ts], 1))
        high, low = split(jnp.concatenate(parts, 0))
        x = dot(high, th) + dot(low, th) + dot(high, tl)
        return x[:, :width], x[:, width:]

    def stream(s):
        return sent_ref[:, s * chans : (s + 1) * chans].astype(jnp.float32)

    def put(s, x):
        half = blocks // 2
        for i in range(blocks):
            at = i % half
            out_ref[i // half, s * chans : (s + 1) * chans, at * width : (at + 1) * width] = x[i].astype(jnp.bfloat16)

    gate = flat((stream(1) * stream(2)).astype(jnp.bfloat16).astype(jnp.float32)).astype(jnp.bfloat16)
    carr = flat((stream(3) * stream(0)).astype(jnp.bfloat16).astype(jnp.float32)).astype(jnp.bfloat16)
    filt = jnp.stack([filt_ref[:, i * width : (i + 1) * width] for i in range(blocks)], 0)
    fr, fi = forward(*split(flat(filt)))
    gr, gi = forward(gate, None)
    cr, ci = forward(carr, None)
    for ref, parts in ((gate_ref, (gr, gi)), (carr_ref, (cr, ci))):
        ref[:, :width] = parts[0]
        ref[:, width:] = parts[1]
    tables = (li, tc, ts, uh, ul)
    conv = inverse(fr * gr - fi * gi, fr * gi + fi * gr, chans, width, tables).astype(jnp.bfloat16).astype(jnp.float32)
    put(0, stream(3) * conv)
    back = inverse(fr * cr + fi * ci, fr * ci - fi * cr, chans, width, tables).astype(jnp.bfloat16).astype(jnp.float32)
    put(1, back * stream(2))
    put(2, back * stream(1))


def vmem_call(body, outs, *args, scratch=(), place=None, away=()):
    specs = [pl.BlockSpec(memory_space=pltpu.VMEM)] * len(args)
    if place is not None:
        specs = [pl.BlockSpec(memory_space=pltpu.SMEM)] + specs
        args = (place,) + args
    return pl.pallas_call(
        body,
        out_shape=tuple(jax.ShapeDtypeStruct(shape, dtype) for shape, dtype in outs),
        in_specs=specs,
        out_specs=tuple(pl.BlockSpec(memory_space=pl.ANY if k in away else pltpu.VMEM) for k in range(len(outs))),
        scratch_shapes=scratch,
        compiler_params=pltpu.CompilerParams(vmem_limit_bytes=24 * 1024 * 1024),
    )(*args)


def spectral(sent, filters):
    blocks, _, width = sent.shape
    chans = filters.shape[0]
    values = tables(blocks, width)
    spectrum = ((chans * values[2].shape[0], 2 * width), jnp.float32)
    return vmem_call(
        functools.partial(kernel, chans, width, blocks),
        [((2, 3 * chans, blocks * width // 2), jnp.bfloat16), spectrum, spectrum],
        sent,
        filters,
        *values,
    )


def filter_taps(gate, carr, chans, blocks):
    width = gate.shape[1] // 2
    _, li, tc, ts, _, _, uh, ul = tables(blocks, width)
    return vmem_call(
        functools.partial(taps_kernel, chans, width, blocks),
        [((chans, blocks * width), jnp.float32)],
        gate,
        carr,
        li,
        tc,
        ts,
        uh,
        ul,
    )[0]


def pack_kernel(chans, inputs_ref, projected_ref, grad_ref, out_ref, sems):
    copies = [
        pltpu.make_async_copy(projected_ref.at[s], out_ref.at[:, s * chans : (s + 1) * chans], sems.at[s])
        for s in range(3)
    ]
    copies.append(pltpu.make_async_copy(grad_ref, out_ref.at[:, 3 * chans : 4 * chans], sems.at[3]))
    copies.append(pltpu.make_async_copy(inputs_ref.at[:, lax.axis_index("x")], out_ref.at[:, 4 * chans :], sems.at[4]))
    for copy in copies:
        copy.start()
    for copy in copies:
        copy.wait()


def chunk(place_ref, blocks, ry, rc):
    y, z, c = place_ref[0], place_ref[1], place_ref[2]
    half = lax.rem(y + ry, 2)
    at = pl.multiple_of((2 * z + lax.rem(c + rc, 2)) * 128, 128)
    return jnp.concatenate([block[half, :, pl.ds(at, 128)] for block in blocks], 0)


def stack_kernel(*refs):
    blocks, out_ref = refs[:-1], refs[-1]
    count = out_ref.shape[1] // len(blocks)
    for k, block in enumerate(blocks):
        out_ref[:, k * count : (k + 1) * count] = block[...]


def product_kernel(place_ref, *refs):
    if len(refs) > 10:
        own, first, second, third, other, other_first, other_second, other_third = refs[:8]
        blocks, outs, x_ref = refs[8:-5], refs[-5:-1], refs[-1]
        _, steps, part, width = own.shape
        for rc, pieces in enumerate(((own, first, third, other_second), (other, second, other_third, other_first))):
            for ry in range(2):
                for k, ref in enumerate(pieces):
                    row = ((2 * rc + ry) * 4 + k) * part
                    for i in range(steps):
                        x_ref[row : row + part, i * width : (i + 1) * width] = ref[ry, i]
    else:
        x_ref, blocks, outs = refs[0], refs[1:-4], refs[-4:]
    halves = [jnp.concatenate([block[h] for block in blocks], 0) for h in range(2)]
    rows, length = halves[0].shape
    size = x_ref.shape[0] // 4
    part = size // 4
    for rc in range(2):
        total = None
        for h in range(2):
            x = x_ref[2 * rc * size : 2 * (rc + 1) * size, h * length : (h + 1) * length]
            got = lax.dot_general(halves[h], x, (((1,), (1,)), ((), ())), preferred_element_type=jnp.float32)
            total = got if total is None else total + got
        for ry in range(2):
            t = total[:, ry * size : (ry + 1) * size]
            u = jnp.concatenate([t[:, :part], t[:, 3 * part :], t[:, 2 * part : 3 * part], t[:, part : 2 * part]], 1)
            out_ref = outs[2 * ry + rc]
            out_ref[:rows] = jnp.where(place_ref[2] == 0, u, t).astype(jnp.bfloat16)
            out_ref[rows:] = chunk(place_ref, blocks, ry, rc)


def finish_kernel(chans, n, slots, place_ref, *refs):
    groups, (proj_out, weight_out, proj_ref, weight_ref, turned_ref, sems) = refs[:-6], refs[-6:]
    y, z, c, x = (place_ref[k] for k in range(4))
    for g, slot_list in enumerate(slots):
        rows = 3 * chans * len(slot_list)
        for near in range(4):
            ref = groups[4 * g + near]
            core = lax.rem(c + near % 2, 2)
            row_y = lax.rem(y + near // 2, 2) * 2 * n
            for m, (hops, turned) in enumerate(slot_list):
                owner = row_y + 2 * lax.rem(z + n - hops + 2 * hops * core, n) + (1 - core if turned else core)
                at = pl.multiple_of(owner * chans, chans)
                for s in range(3):
                    row = (3 * m + s) * chans
                    turned_ref[s, pl.ds(at, chans), :] = ref[row : row + chans, :].astype(jnp.float32)
                    proj_ref[s, pl.ds(at, chans), :] = ref[rows + row : rows + row + chans, :]
    copies = [pltpu.make_async_copy(proj_ref, proj_out, sems.at[3])]
    copies[0].start()
    n_x = 4
    part = weight_ref.shape[1] // n_x
    for s in range(3):
        rows = turned_ref[s].T
        for k in range(n_x):
            at = pl.multiple_of(lax.rem(x + k, n_x) * part, part)
            weight_ref[s, pl.ds(at, part), :] = rows[k * part : (k + 1) * part]
        copies.append(pltpu.make_async_copy(weight_ref.at[s], weight_out.at[s], sems.at[s]))
        copies[-1].start()
    for copy in copies:
        copy.wait()


def spread(x, axis):
    n = lax.axis_size(axis)
    perm = [(2 * i, 2 * ((i + 1) % n)) for i in range(n)] + [(2 * i + 1, 2 * ((i + n - 1) % n) + 1) for i in range(n)]
    return lax.ppermute(x, (axis, "core"), perm)


def swap(x, axis):
    return lax.ppermute(x, axis, [(0, 1), (1, 0)])


def after(x, *others):
    return lax.optimization_barrier((x, *others))[0]


def trade(parts):
    across = lax.ppermute(parts[3], ("ylo", "core"), [(0, 3), (1, 2), (2, 1), (3, 0)])
    return parts[0], swap(parts[1], "core"), swap(parts[2], "ylo"), across


def local(inputs, projected, filters, grad_out):
    count, width = grad_out.shape
    chans = filters.shape[0]
    owners = count // chans
    n = lax.axis_size("z")
    n_x = lax.axis_size("x")
    bf16 = jnp.bfloat16
    place = jnp.stack([lax.axis_index(a) for a in ("ylo", "z", "core", "x")]).astype(jnp.int32)
    rows = inputs.shape[0] // (owners * n_x)

    sent = pl.pallas_call(
        functools.partial(pack_kernel, chans),
        out_shape=jax.ShapeDtypeStruct((owners, 4 * chans + rows, width), bf16),
        in_specs=[pl.BlockSpec(memory_space=pl.ANY)] * 3,
        out_specs=pl.BlockSpec(memory_space=pltpu.VMEM),
        scratch_shapes=[pltpu.SemaphoreType.DMA((5,))],
    )(
        inputs.reshape(owners, n_x, rows, width),
        projected.reshape(3, owners, chans, width),
        grad_out.reshape(owners, chans, width),
    )
    sent = lax.all_to_all(sent, SEQ, split_axis=0, concat_axis=0, tiled=True)
    own_rows = sent[:, 4 * chans :]
    sent, own_rows = lax.optimization_barrier((sent, own_rows))
    y_rows = swap(own_rows, "ylo")

    block, gate, carr = spectral(sent, filters)
    filter_grad = filter_taps(gate, carr, chans, owners)
    a1 = spread(block, "z")
    turned = swap(block, "core")
    turned = after(turned, block)
    b1 = spread(turned, "z")
    a2 = spread(after(a1, turned), "z")
    b2 = spread(after(b1, a1), "z")
    both_rows = jnp.stack([own_rows, after(y_rows, a1)])
    other_rows = swap(both_rows, "core")
    xa1 = spread(both_rows, "x")
    xb1 = spread(after(other_rows, b1), "x")
    a3 = spread(after(a2, b1), "z")
    b3 = spread(after(b2, a2), "z")
    xa2 = spread(after(xa1, b1), "x")
    (first,) = vmem_call(stack_kernel, [((2, 6 * block.shape[1], block.shape[2]), bf16)], block, a1, b1, a2, b2, b3)
    a4 = spread(after(a3, b2), "z")

    slots = (((0, 0), (1, 0), (1, 1), (2, 0), (2, 1), (3, 1)), ((3, 0), (4, 0)))
    fa1 = swap(after(xa1, a3), "core")
    fb1 = swap(after(xb1, a3), "core")
    fa2 = swap(after(xa2, first), "core")
    pieces = (both_rows, xa1, xb1, xa2, other_rows, fa1, fb1, fa2)
    *parts, whole = vmem_call(
        product_kernel,
        [((2 * first.shape[1], width), bf16)] * 4 + [((4 * n_x * rows, owners * width), bf16)],
        *pieces,
        first,
        place=place,
    )
    groups = trade(parts)
    a3, a4 = lax.optimization_barrier((a3, a4, parts[0]))[:2]
    parts = vmem_call(product_kernel, [((4 * a4.shape[1], width), bf16)] * 4, whole, a3, a4, place=place)
    groups += trade(parts)
    proj_grad, weight_grad = vmem_call(
        functools.partial(finish_kernel, chans, n, slots),
        [((3, count, width), bf16), ((3, n_x * rows, count), jnp.float32)],
        *groups,
        scratch=[
            pltpu.VMEM((3, count, width), bf16),
            pltpu.VMEM((3, n_x * rows, count), jnp.float32),
            pltpu.VMEM((3, count, width), jnp.float32),
            pltpu.SemaphoreType.DMA((4,)),
        ],
        away=(0, 1),
        place=place,
    )
    return proj_grad, weight_grad.transpose(1, 0, 2), filter_grad


def solution(mesh):
    fine = Mesh(mesh.devices.reshape(2, 4, 2, 8, 2), ("yhi", "x", "ylo", "z", "core"))
    tp = ("yhi", "x")
    in_specs = (P(None, SEQ), P(None, tp, SEQ), P(tp + SEQ, None), P(tp, SEQ))
    out_specs = (P(None, tp, SEQ), P(SEQ, None, tp), P(tp + SEQ, None))
    return jax.shard_map(local, mesh=fine, in_specs=in_specs, out_specs=out_specs, check_vma=False)
```
